512 devices in a mesh: replica: 64 (over y, z), fsdp: 8 (over x, core).
Axes of the slice: x: 4, y: 8, z: 8, core: 2. Of those that a mesh axis runs over, the one named last changes fastest.
Arguments:
- replica_params: bfloat16 [64, 2, 128, 8192], P('replica', None, 'fsdp'), may hold values from -1.1 to 1.1
- outer_base: float32 [2, 128, 8192], P(None, 'fsdp'), may hold values from -1 to 1
- outer_momentum: float32 [2, 128, 8192], P(None, 'fsdp', 'replica'), may hold values from -0.012 to 0.012
Outputs:
- new_base: float32 [2, 128, 8192], P(None, 'fsdp')
- new_momentum: float32 [2, 128, 8192], P(None, 'fsdp', 'replica')
The draws below stay inside these ranges and needn't reach their ends.
All inputs are finite; a program needn't handle non-finite values.
Results may differ from the reference program's by a relative error of at most 0.0023.
Values may be sent and summed in bfloat16 or wider, within the bound.
No kernel may reach another device: no remote copies, remote signals or barrier semaphores. Data moves between devices by JAX's collectives and lax.ppermute only.
A program may use at most 64 MiB of HBM per device.

```python
import math
import jax
import jax.numpy as jnp
from jax import lax

D = 8192
BLOCK = 128
LAYERS = 2
ROWS = 128
REPLICAS = 64
N_REPLICA = 64


def base_field(key, spread):
    first, second, third = jax.random.split(jax.random.fold_in(key, 101), 3)
    entries = jax.random.truncated_normal(first, -4.0, 4.0, (LAYERS, ROWS, D), jnp.float32)
    column_scale = jnp.power(10.0, jax.random.uniform(second, (D,), jnp.float32, -spread, spread))
    row_scale = jnp.power(10.0, jax.random.uniform(third, (ROWS,), jnp.float32, -spread, spread))
    return 0.02 * entries * row_scale[None, :, None] * column_scale[None, None, :]


def draw_outer_base(key, part):
    return base_field(key, 0.5)


def draw_replica_params(key, part):
    base = base_field(key, 0.5)
    key = jax.random.fold_in(key, 23)
    first, second, third, fourth = jax.random.split(key, 4)
    layer_scale = jnp.exp(jax.random.uniform(first, (LAYERS,), jnp.float32, jnp.log(0.0015), jnp.log(0.004)))
    column_factor = jnp.power(10.0, jax.random.uniform(second, (D,), jnp.float32, -0.5, 0.5))
    rising = 1.0 + 2.0 * jnp.arange(REPLICAS, dtype=jnp.float32) / (REPLICAS - 1)
    common = jax.random.truncated_normal(third, -4.0, 4.0, (LAYERS, ROWS, D), jnp.float32)
    own = jax.random.truncated_normal(fourth, -4.0, 4.0, (REPLICAS, LAYERS, ROWS, D), jnp.float32)
    common_drift = common * layer_scale[:, None, None] * column_factor[None, None, :]
    own_drift = 0.001 * own * rising[:, None, None, None] * column_factor[None, None, None, :]
    return (base[None] + common_drift[None] + own_drift).astype(jnp.bfloat16)


def steps_of(key, shape, cuts, low, top_value):
    def one(dim, parts):
        heights = jax.random.uniform(jax.random.fold_in(jax.random.fold_in(key, 6), dim), (parts,), jnp.float32, low / len(cuts), top_value / len(cuts))
        return jnp.repeat(jnp.exp(heights), shape[dim] // parts).reshape((-1,) + (1,) * (len(shape) - dim - 1))

    gain = one(*cuts[0])
    for cut in cuts[1:]:
        gain = gain * one(*cut)
    return gain


def noise(rng, shape, deviation, bound, shards=(), kind=jnp.bfloat16):
    loudness = steps_of(rng, shape, shards, -0.22, 0.18) if shards else 1.0
    drawn = jax.random.normal(rng, shape, jnp.float32) * deviation * loudness
    return jnp.minimum(jnp.maximum(drawn, -bound), bound).astype(kind)


def setup_inputs(seed: int = 0) -> dict:
    key_list = jax.random.split(jax.random.key(seed), 4)
    return {
        "replica_params": draw_replica_params(jax.random.fold_in(key_list[3], 71), 0),
        "outer_base": draw_outer_base(jax.random.fold_in(key_list[3], 71), 0),
        "outer_momentum": noise(key_list[2], (LAYERS, ROWS, D), 0.002, 0.012, ((1, 8), (2, 64)), jnp.float32),
    }


CODE_RANGE = 448.0
EPSILON = 1e-06
OUTER_RATE = 0.7
NESTEROV = 0.9
CLIP_RMS = 0.001

def encode(difference):
    blocks = difference.reshape(difference.shape[:-1] + (difference.shape[-1] // BLOCK, BLOCK))
    largest = lax.optimization_barrier(jnp.max(jnp.abs(blocks), axis=-1, keepdims=True))
    scales = ((largest + EPSILON) / CODE_RANGE).astype(jnp.bfloat16)
    code_words = (blocks / scales.astype(jnp.float32)).astype(jnp.bfloat16)
    return lax.optimization_barrier((code_words, scales))

def decode(code_words, scales):
    restored = code_words.astype(jnp.float32) * scales.astype(jnp.float32)
    return restored.reshape(restored.shape[:-2] + (restored.shape[-2] * restored.shape[-1],))

def reference(replica_params, outer_base, outer_momentum):

    def accumulate(summed, sample):
        difference = outer_base - sample.astype(jnp.float32)
        code_words, scales = encode(difference)
        return (summed + decode(code_words, scales), None)
    start = jnp.zeros(outer_base.shape, jnp.float32)
    summed, _ = lax.scan(accumulate, start, replica_params)
    averaged = summed / N_REPLICA
    square_sum = lax.optimization_barrier(jnp.sum(averaged * averaged, axis=(1, 2)))
    limit = CLIP_RMS * math.sqrt(ROWS * D)
    factor = jnp.minimum(1.0, limit / (jnp.sqrt(square_sum) + EPSILON))[:, None, None]
    clipped = averaged * factor
    new_momentum = NESTEROV * outer_momentum + clipped
    outer_step = lax.optimization_barrier((OUTER_RATE * (clipped + NESTEROV * new_momentum)).astype(jnp.bfloat16))
    new_base = outer_base - outer_step.astype(jnp.float32)
    return (new_base, new_momentum)
```

```python
import math

import jax
import jax.numpy as jnp
from jax import lax
from jax.experimental import pallas as pl
from jax.sharding import PartitionSpec as P

BLOCK = 128


CODE_RANGE = 448.0
EPSILON = 1e-06
OUTER_RATE = 0.7
NESTEROV = 0.9
CLIP_RMS = 0.001


def split_kernel(params_ref, blocks_ref):
    replicas, layers, rows, width = blocks_ref.shape
    for replica in range(replicas):
        blocks_ref[replica] = params_ref[0, :, :, pl.ds(replica * width, width)]


def average_kernel(received_ref, base_ref, averaged_ref, square_ref):
    replicas = received_ref.shape[0]
    layers, rows, width = base_ref.shape
    base = base_ref[...].reshape(layers * rows, width)

    def accumulate(replica, summed):
        difference = base - received_ref[replica].reshape(layers * rows, width).astype(jnp.float32)
        largest = jnp.max(jnp.abs(difference), axis=-1, keepdims=True)
        scales = ((largest + EPSILON) / CODE_RANGE).astype(jnp.bfloat16).astype(jnp.float32)
        code_words = (difference / scales).astype(jnp.bfloat16)
        return summed + code_words.astype(jnp.float32) * scales

    summed = lax.fori_loop(
        0, replicas, accumulate, jnp.zeros((layers * rows, width), jnp.float32), unroll=8
    )
    averaged = summed / replicas
    averaged_ref[...] = averaged.reshape(layers, rows, width)
    squares = (averaged * averaged).reshape(layers, rows, width)
    square_sum = jnp.sum(jnp.sum(squares, axis=1), axis=-1, keepdims=True)
    for layer in range(layers):
        square_ref[layer : layer + 1] = jnp.broadcast_to(square_sum[layer : layer + 1], (1, width))


def step_kernel(limit, squares_ref, averaged_ref, momentum_ref, momentum_next_ref, step_ref):
    layers, rows, width = averaged_ref.shape
    sums = jnp.sum(squares_ref[...], axis=0, keepdims=True)
    share = width // layers
    for layer in range(layers):
        total = jnp.max(sums[:, layer * share : (layer + 1) * share], axis=-1, keepdims=True)
        factor = jnp.minimum(1.0, limit / (jnp.sqrt(total) + EPSILON))
        clipped = averaged_ref[layer] * factor
        momentum_next = NESTEROV * momentum_ref[layer] + clipped
        momentum_next_ref[layer] = momentum_next
        step = (OUTER_RATE * (clipped + NESTEROV * momentum_next)).astype(jnp.bfloat16)
        for replica in range(step_ref.shape[0]):
            step_ref[replica, layer] = step


def base_kernel(steps_ref, base_ref, new_base_ref):
    replicas, layers, rows, width = steps_ref.shape
    for replica in range(replicas):
        columns = pl.ds(replica * width, width)
        for layer in range(layers):
            step = steps_ref[replica, layer].astype(jnp.float32)
            new_base_ref[layer, :, columns] = base_ref[layer, :, columns] - step


def per_device(replica_params, outer_base, outer_momentum):
    replicas = lax.axis_size("replica")
    owner_index = lax.axis_index("replica")
    everyone = replicas * lax.axis_size("fsdp")
    layers, rows, width = outer_base.shape
    owned = width // replicas
    limit = CLIP_RMS * math.sqrt(rows * lax.axis_size("fsdp") * width)

    blocks = pl.pallas_call(
        split_kernel,
        out_shape=jax.ShapeDtypeStruct((replicas, layers, rows, owned), replica_params.dtype),
        name="split",
    )(replica_params)
    received = lax.all_to_all(blocks, "replica", 0, 0, tiled=True)
    owned_base = lax.dynamic_slice_in_dim(outer_base, owner_index * owned, owned, 2)

    averaged, square_sum = pl.pallas_call(
        average_kernel,
        out_shape=(
            jax.ShapeDtypeStruct((layers, rows, owned), jnp.float32),
            jax.ShapeDtypeStruct((layers, owned), jnp.float32),
        ),
        name="average",
    )(received, owned_base)

    mine = square_sum[:, : owned // layers].reshape(1, 1, owned)
    squares = lax.all_to_all(
        jnp.broadcast_to(mine, (everyone, 1, owned)), ("replica", "fsdp"), 0, 0, tiled=True
    )

    momentum_next, step = pl.pallas_call(
        lambda *refs: step_kernel(limit, *refs),
        out_shape=(
            jax.ShapeDtypeStruct((layers, rows, owned), jnp.float32),
            jax.ShapeDtypeStruct((replicas, layers, rows, owned), jnp.bfloat16),
        ),
        name="step",
    )(squares.reshape(everyone, owned), averaged, outer_momentum)

    steps = lax.all_to_all(step, "replica", 0, 0, tiled=True)
    new_base = pl.pallas_call(
        base_kernel,
        out_shape=jax.ShapeDtypeStruct((layers, rows, width), jnp.float32),
        name="base",
    )(steps, outer_base)
    return (new_base, momentum_next)


def solution(mesh):
    placed = (P("replica", None, "fsdp", None), P(None, "fsdp", None), P(None, "fsdp", "replica"))
    return jax.shard_map(
        per_device,
        mesh=mesh,
        in_specs=placed,
        out_specs=(P(None, "fsdp", None), P(None, "fsdp", "replica")),
        check_vma=False,
    )
```

```python
import math

import jax
import jax.numpy as jnp
from jax import lax
from jax.experimental import pallas as pl
from jax.experimental.pallas import tpu as pltpu
from jax.sharding import Mesh, PartitionSpec as P

BLOCK = 128


CODE_RANGE = 448.0
EPSILON = 1e-06
OUTER_RATE = 0.7
NESTEROV = 0.9
CLIP_RMS = 0.001
SUBLANES = 8
VMEM_LIMIT = 8 * 2**20


def split_kernel(params_ref, blocks_ref, semaphores):
    copies = [
        pltpu.make_async_copy(params_ref.at[group], blocks_ref.at[:, group], semaphores.at[group])
        for group in range(params_ref.shape[0])
    ]
    for copy in copies:
        copy.start()
    for copy in copies:
        copy.wait()


def average_kernel(received_ref, base_ref, averaged_ref, square_ref):
    replicas = received_ref.shape[0]
    base = base_ref[...]

    def accumulate(replica, summed):
        difference = base - received_ref[replica].astype(jnp.float32)
        largest = jnp.max(jnp.abs(difference), axis=-1, keepdims=True)
        scales = ((largest + EPSILON) / CODE_RANGE).astype(jnp.bfloat16).astype(jnp.float32)
        code_words = (difference / scales).astype(jnp.bfloat16)
        return summed + code_words.astype(jnp.float32) * scales

    summed = lax.fori_loop(0, replicas, accumulate, jnp.zeros(base.shape, jnp.float32), unroll=8)
    averaged = summed / replicas
    averaged_ref[...] = averaged
    squares = averaged * averaged
    half = squares.shape[0] // 2
    first = jnp.sum(jnp.sum(jnp.sum(squares[:half], axis=0), axis=0, keepdims=True), axis=-1, keepdims=True)
    second = jnp.sum(jnp.sum(jnp.sum(squares[half:], axis=0), axis=0, keepdims=True), axis=-1, keepdims=True)
    lanes = lax.broadcasted_iota(jnp.int32, square_ref.shape, 1)
    square_ref[...] = jnp.where(lanes < BLOCK // 2, first, second)


def pack_kernel(squares_ref, averaged_ref, momentum_ref, packed_ref):
    sums = jnp.broadcast_to(jnp.sum(squares_ref[...], axis=0, keepdims=True), (SUBLANES, BLOCK))
    groups = averaged_ref.shape[0]
    for peer in range(packed_ref.shape[0]):
        for group in range(groups):
            packed_ref[peer, group] = averaged_ref[group]
            packed_ref[peer, groups + group] = momentum_ref[group]
        packed_ref[peer, 2 * groups] = sums


def step_kernel(limit, packed_ref, averaged_ref, momentum_ref, momentum_next_ref, step_ref):
    peers = packed_ref.shape[0]
    groups = averaged_ref.shape[0]
    sums = packed_ref[0, 2 * groups]
    for peer in range(1, peers):
        sums = sums + packed_ref[peer, 2 * groups]
    factors = []
    for layer in range(2):
        total = jnp.max(sums[:, layer * 64 : (layer + 1) * 64], axis=-1, keepdims=True)
        factors.append(jnp.minimum(1.0, limit / (jnp.sqrt(total) + EPSILON)))
    for group in range(groups):
        factor = factors[group * 2 // groups]
        momentum_next_ref[group] = NESTEROV * momentum_ref[group] + averaged_ref[group] * factor
        for peer in range(peers):
            clipped = packed_ref[peer, group] * factor
            momentum_next = NESTEROV * packed_ref[peer, groups + group] + clipped
            step = (OUTER_RATE * (clipped + NESTEROV * momentum_next)).astype(jnp.bfloat16)
            for target in range(step_ref.shape[0]):
                step_ref[target, peer, group] = step


def base_kernel(steps_ref, base_ref, new_base_ref):
    owners, groups = steps_ref.shape[:2]
    layers = base_ref.shape[0]
    for owner in range(owners):
        columns = pl.ds(owner * BLOCK, BLOCK)
        for group in range(groups):
            layer, part = divmod(group, groups // layers)
            rows = pl.ds(part * SUBLANES, SUBLANES)
            step = steps_ref[owner, group].astype(jnp.float32)
            new_base_ref[layer, rows, columns] = base_ref[layer, rows, columns] - step


def per_device(replica_params, outer_base, outer_momentum):
    ys, zs = lax.axis_size("y"), lax.axis_size("z")
    replicas = ys * zs
    fsdp = lax.axis_size("fsdp")
    layers, rows, width = outer_base.shape
    groups = layers * rows // SUBLANES
    limit = CLIP_RMS * math.sqrt(rows * fsdp * width)
    owner_index = lax.axis_index("y") * zs + lax.axis_index("z")
    params = pltpu.CompilerParams(vmem_limit_bytes=VMEM_LIMIT)
    tile = (groups, SUBLANES, BLOCK)

    grouped = replica_params.reshape(groups, SUBLANES, replicas, BLOCK).transpose(0, 2, 1, 3)
    blocks = pl.pallas_call(
        split_kernel,
        out_shape=jax.ShapeDtypeStruct((replicas, *tile), replica_params.dtype),
        in_specs=[pl.BlockSpec(memory_space=pl.ANY)],
        out_specs=pl.BlockSpec(memory_space=pl.ANY),
        scratch_shapes=[pltpu.SemaphoreType.DMA((groups,))],
        compiler_params=pltpu.CompilerParams(vmem_limit_bytes=60 * 2**20),
        name="split",
    )(grouped)
    received = lax.all_to_all(blocks, ("y", "z"), 0, 0, tiled=True)
    owned_base = lax.dynamic_slice_in_dim(outer_base, owner_index * BLOCK, BLOCK, 2).reshape(tile)
    momentum = outer_momentum.reshape(tile)

    averaged, squares = pl.pallas_call(
        average_kernel,
        out_shape=(
            jax.ShapeDtypeStruct(tile, jnp.float32),
            jax.ShapeDtypeStruct((ys * fsdp, BLOCK), jnp.float32),
        ),
        compiler_params=params,
        name="average",
    )(received, owned_base)

    squares = lax.all_to_all(
        squares.reshape(ys * fsdp, 1, BLOCK), ("y", "fsdp"), 0, 0, tiled=True
    ).reshape(ys * fsdp, BLOCK)
    packed = pl.pallas_call(
        pack_kernel,
        out_shape=jax.ShapeDtypeStruct((zs, 2 * groups + 1, SUBLANES, BLOCK), jnp.float32),
        compiler_params=params,
        name="pack",
    )(squares, averaged, momentum)
    packed = lax.all_to_all(packed, "z", 0, 0, tiled=True)

    momentum_next, step = pl.pallas_call(
        lambda *refs: step_kernel(limit, *refs),
        out_shape=(
            jax.ShapeDtypeStruct(tile, jnp.float32),
            jax.ShapeDtypeStruct((ys, zs, *tile), jnp.bfloat16),
        ),
        compiler_params=params,
        name="step",
    )(packed, averaged, momentum)

    steps = lax.all_to_all(step, "y", 0, 0, tiled=True).reshape(replicas, *tile)
    chunks = 4
    new_base = pl.pallas_call(
        base_kernel,
        grid=(chunks,),
        in_specs=[
            pl.BlockSpec((replicas // chunks, *tile), lambda i: (i, 0, 0, 0)),
            pl.BlockSpec((layers, rows, width // chunks), lambda i: (0, 0, i)),
        ],
        out_specs=pl.BlockSpec((layers, rows, width // chunks), lambda i: (0, 0, i)),
        out_shape=jax.ShapeDtypeStruct((layers, rows, width), jnp.float32),
        compiler_params=params,
        name="base",
    )(steps, outer_base)
    return (new_base, momentum_next.reshape(outer_momentum.shape))


def solution(mesh):
    replicas, fsdp = mesh.devices.shape
    side = math.isqrt(replicas)
    torus = Mesh(mesh.devices.reshape(side, side, fsdp), ("y", "z", "fsdp"))
    return jax.shard_map(
        per_device,
        mesh=torus,
        in_specs=(
            P(("y", "z"), None, "fsdp", None),
            P(None, "fsdp", None),
            P(None, "fsdp", ("y", "z")),
        ),
        out_specs=(P(None, "fsdp", None), P(None, "fsdp", ("y", "z"))),
        check_vma=False,
    )
```

```python
import math

import jax
import jax.numpy as jnp
from jax import lax
from jax.experimental import pallas as pl
from jax.experimental.pallas import tpu as pltpu
from jax.sharding import Mesh, PartitionSpec as P

BLOCK = 128


CODE_RANGE = 448.0
EPSILON = 1e-06
OUTER_RATE = 0.7
NESTEROV = 0.9
CLIP_RMS = 0.001
SUBLANES = 8
VMEM_LIMIT = 8 * 2**20


def split_kernel(params_ref, blocks_ref):
    for owner in range(blocks_ref.shape[0]):
        blocks_ref[owner] = params_ref[:, owner]


def partial_kernel(received_ref, base_ref, momentum_ref, packed_ref):
    sources, blocks, groups = received_ref.shape[:3]
    layers = base_ref.shape[0]
    peers = packed_ref.shape[0]
    for block in range(blocks):
        columns = pl.ds(block * BLOCK, BLOCK)
        base = base_ref[:, :, columns].reshape(groups, SUBLANES, BLOCK)
        summed = jnp.zeros(base.shape, jnp.float32)
        for source in range(sources):
            difference = base - received_ref[source, block].astype(jnp.float32)
            largest = jnp.max(jnp.abs(difference), axis=-1, keepdims=True)
            scales = ((largest + EPSILON) / CODE_RANGE).astype(jnp.bfloat16).astype(jnp.float32)
            code_words = (difference / scales).astype(jnp.bfloat16)
            summed = summed + code_words.astype(jnp.float32) * scales
        sent = summed.astype(jnp.bfloat16)
        for peer in range(peers):
            packed_ref[peer, block] = sent
    momentum = momentum_ref[...].astype(jnp.bfloat16)
    for peer in range(peers):
        packed_ref[peer, blocks] = momentum


def average_kernel(replicas, packed_ref, averaged_ref, square_ref):
    sources = packed_ref.shape[0]
    blocks, groups = averaged_ref.shape[:2]
    squares = jnp.zeros((groups, SUBLANES, BLOCK), jnp.float32)
    for block in range(blocks):
        summed = packed_ref[0, block].astype(jnp.float32)
        for source in range(1, sources):
            summed = summed + packed_ref[source, block].astype(jnp.float32)
        averaged = summed / replicas
        averaged_ref[block] = averaged
        squares = squares + averaged * averaged
    half = groups // 2
    first = jnp.sum(jnp.sum(jnp.sum(squares[:half], axis=0), axis=0, keepdims=True), axis=-1, keepdims=True)
    second = jnp.sum(jnp.sum(jnp.sum(squares[half:], axis=0), axis=0, keepdims=True), axis=-1, keepdims=True)
    lanes = lax.broadcasted_iota(jnp.int32, square_ref.shape, 1)
    square_ref[...] = jnp.where(lanes < BLOCK // 2, first, second)


def step_kernel(limit, mine_ref, squares_ref, averaged_ref, packed_ref, momentum_ref, momentum_next_ref, step_ref):
    blocks, groups = averaged_ref.shape[:2]
    sums = jnp.sum(squares_ref[...], axis=0, keepdims=True)
    mine = mine_ref[0]
    for group in range(groups):
        layer = group * 2 // groups
        total = jnp.max(sums[:, layer * 64 : (layer + 1) * 64], axis=-1, keepdims=True)
        factor = jnp.minimum(1.0, limit / (jnp.sqrt(total) + EPSILON))
        momentum_next_ref[group] = NESTEROV * momentum_ref[group] + averaged_ref[mine, group] * factor
        for block in range(blocks):
            clipped = averaged_ref[block, group] * factor
            momentum_next = NESTEROV * packed_ref[block, blocks, group].astype(jnp.float32) + clipped
            step = (OUTER_RATE * (clipped + NESTEROV * momentum_next)).astype(jnp.bfloat16)
            for target in range(step_ref.shape[0]):
                step_ref[target, block, group] = step


def base_kernel(steps_ref, base_ref, new_base_ref):
    owners, groups = steps_ref.shape[:2]
    layers = base_ref.shape[0]
    for owner in range(owners):
        columns = pl.ds(owner * BLOCK, BLOCK)
        for group in range(groups):
            layer, part = divmod(group, groups // layers)
            rows = pl.ds(part * SUBLANES, SUBLANES)
            step = steps_ref[owner, group].astype(jnp.float32)
            new_base_ref[layer, rows, columns] = base_ref[layer, rows, columns] - step


def per_device(replica_params, outer_base, outer_momentum):
    ys, zs = lax.axis_size("y"), lax.axis_size("z")
    replicas = ys * zs
    fsdp = lax.axis_size("fsdp")
    layers, rows, width = outer_base.shape
    groups = layers * rows // SUBLANES
    limit = CLIP_RMS * math.sqrt(rows * fsdp * width)
    params = pltpu.CompilerParams(vmem_limit_bytes=VMEM_LIMIT)
    tile = (groups, SUBLANES, BLOCK)

    grouped = replica_params.reshape(groups, SUBLANES, replicas, BLOCK).transpose(0, 2, 1, 3)
    blocks = pl.pallas_call(
        split_kernel,
        out_shape=jax.ShapeDtypeStruct((replicas, *tile), replica_params.dtype),
        compiler_params=params,
        name="split",
    )(grouped)
    received = lax.all_to_all(blocks.reshape(ys, zs, *tile), "y", 0, 0, tiled=True)
    columns = zs * BLOCK
    owned_base = lax.dynamic_slice_in_dim(outer_base, lax.axis_index("y") * columns, columns, 2)
    momentum = outer_momentum.reshape(tile)

    packed = pl.pallas_call(
        partial_kernel,
        out_shape=jax.ShapeDtypeStruct((zs, zs + 1, *tile), jnp.bfloat16),
        compiler_params=params,
        name="partial",
    )(received, owned_base, momentum)
    packed = lax.all_to_all(packed, "z", 0, 0, tiled=True)

    averaged, squares = pl.pallas_call(
        lambda *refs: average_kernel(replicas, *refs),
        out_shape=(
            jax.ShapeDtypeStruct((zs, *tile), jnp.float32),
            jax.ShapeDtypeStruct((ys * fsdp, BLOCK), jnp.float32),
        ),
        compiler_params=params,
        name="average",
    )(packed)
    squares = lax.all_to_all(
        squares.reshape(ys * fsdp, 1, BLOCK), ("y", "fsdp"), 0, 0, tiled=True
    ).reshape(ys * fsdp, BLOCK)

    vmem = pl.BlockSpec(memory_space=pltpu.VMEM)
    momentum_next, step = pl.pallas_call(
        lambda *refs: step_kernel(limit, *refs),
        in_specs=[pl.BlockSpec(memory_space=pltpu.SMEM), vmem, vmem, vmem, vmem],
        out_shape=(
            jax.ShapeDtypeStruct(tile, jnp.float32),
            jax.ShapeDtypeStruct((ys, zs, *tile), jnp.bfloat16),
        ),
        compiler_params=params,
        name="step",
    )(lax.axis_index("z").reshape(1), squares, averaged, packed, momentum)

    steps = lax.all_to_all(step, "y", 0, 0, tiled=True).reshape(replicas, *tile)
    chunks = 4
    new_base = pl.pallas_call(
        base_kernel,
        grid=(chunks,),
        in_specs=[
            pl.BlockSpec((replicas // chunks, *tile), lambda i: (i, 0, 0, 0)),
            pl.BlockSpec((layers, rows, width // chunks), lambda i: (0, 0, i)),
        ],
        out_specs=pl.BlockSpec((layers, rows, width // chunks), lambda i: (0, 0, i)),
        out_shape=jax.ShapeDtypeStruct((layers, rows, width), jnp.float32),
        compiler_params=params,
        name="base",
    )(steps, outer_base)
    return (new_base, momentum_next.reshape(outer_momentum.shape))


def solution(mesh):
    replicas, fsdp = mesh.devices.shape
    side = math.isqrt(replicas)
    torus = Mesh(mesh.devices.reshape(side, side, fsdp), ("y", "z", "fsdp"))
    return jax.shard_map(
        per_device,
        mesh=torus,
        in_specs=(
            P(("y", "z"), None, "fsdp", None),
            P(None, "fsdp", None),
            P(None, "fsdp", ("y", "z")),
        ),
        out_specs=(P(None, "fsdp", None), P(None, "fsdp", ("y", "z"))),
        check_vma=False,
    )
```

```python
import math

import jax
import jax.numpy as jnp
from jax import lax
from jax.experimental import pallas as pl
from jax.experimental.pallas import tpu as pltpu
from jax.sharding import Mesh, PartitionSpec as P

BLOCK = 128


CODE_RANGE = 448.0
EPSILON = 1e-06
OUTER_RATE = 0.7
NESTEROV = 0.9
CLIP_RMS = 0.001
SUBLANES = 8
VMEM_LIMIT = 8 * 2**20


def split_kernel(params_ref, blocks_ref, held_ref, semaphores):
    ys, lows, highs = blocks_ref.shape[:3]
    share = highs * lows
    copies = [
        pltpu.make_async_copy(
            params_ref.at[:, pl.ds(y * share, share)],
            held_ref.at[:, pl.ds(y * share, share)],
            semaphores.at[y],
        )
        for y in range(ys)
    ]
    for copy in copies:
        copy.start()
    for y in range(ys):
        copies[y].wait()
        for low in range(lows):
            for high in range(highs):
                blocks_ref[y, low, high] = held_ref[:, y * share + high * lows + low]


def partial_kernel(place_ref, received_ref, base_ref, momentum_ref, packed_ref):
    sources, blocks, groups = received_ref.shape[:3]
    peers = packed_ref.shape[0]
    for block in range(blocks):
        start = pl.multiple_of((place_ref[0] + block * place_ref[1]) * BLOCK, BLOCK)
        base = base_ref[:, :, pl.ds(start, BLOCK)].reshape(groups, SUBLANES, BLOCK)
        summed = jnp.zeros(base.shape, jnp.float32)
        for source in range(sources):
            difference = base - received_ref[source, block].astype(jnp.float32)
            largest = jnp.max(jnp.abs(difference), axis=-1, keepdims=True)
            scales = ((largest + EPSILON) / CODE_RANGE).astype(jnp.bfloat16).astype(jnp.float32)
            code_words = (difference / scales).astype(jnp.bfloat16)
            summed = summed + code_words.astype(jnp.float32) * scales
        sent = summed.astype(jnp.bfloat16)
        for peer in range(peers):
            packed_ref[peer, block] = sent
    momentum = momentum_ref[...].astype(jnp.bfloat16)
    for peer in range(peers):
        packed_ref[peer, blocks] = momentum


def average_kernel(replicas, packed_ref, averaged_ref, square_ref):
    sources = packed_ref.shape[0]
    blocks, groups = averaged_ref.shape[:2]
    squares = jnp.zeros((groups, SUBLANES, BLOCK), jnp.float32)
    for block in range(blocks):
        summed = packed_ref[0, block].astype(jnp.float32)
        for source in range(1, sources):
            summed = summed + packed_ref[source, block].astype(jnp.float32)
        averaged = summed / replicas
        averaged_ref[block] = averaged
        squares = squares + averaged * averaged
    half = groups // 2
    first = jnp.sum(jnp.sum(jnp.sum(squares[:half], axis=0), axis=0, keepdims=True), axis=-1, keepdims=True)
    second = jnp.sum(jnp.sum(jnp.sum(squares[half:], axis=0), axis=0, keepdims=True), axis=-1, keepdims=True)
    lanes = lax.broadcasted_iota(jnp.int32, square_ref.shape, 1)
    square_ref[...] = jnp.where(lanes < BLOCK // 2, first, second)


def step_kernel(limit, mine_ref, squares_ref, averaged_ref, packed_ref, momentum_ref, momentum_next_ref, step_ref):
    blocks, groups = averaged_ref.shape[:2]
    sums = jnp.sum(squares_ref[...], axis=0, keepdims=True)
    mine = mine_ref[2]
    for group in range(groups):
        layer = group * 2 // groups
        total = jnp.max(sums[:, layer * 64 : (layer + 1) * 64], axis=-1, keepdims=True)
        factor = jnp.minimum(1.0, limit / (jnp.sqrt(total) + EPSILON))
        momentum_next_ref[group] = NESTEROV * momentum_ref[group] + averaged_ref[mine, group] * factor
        for block in range(blocks):
            clipped = averaged_ref[block, group] * factor
            momentum_next = NESTEROV * packed_ref[block, blocks, group].astype(jnp.float32) + clipped
            step = (OUTER_RATE * (clipped + NESTEROV * momentum_next)).astype(jnp.bfloat16)
            for target in range(step_ref.shape[0]):
                step_ref[target, block, group] = step


def base_kernel(steps_ref, base_ref, new_base_ref):
    ys, lows, highs, groups = steps_ref.shape[:4]
    layers = base_ref.shape[0]
    for y in range(ys):
        for high in range(highs):
            for low in range(lows):
                columns = pl.ds(((y * highs + high) * lows + low) * BLOCK, BLOCK)
                for group in range(groups):
                    layer, part = divmod(group, groups // layers)
                    rows = pl.ds(part * SUBLANES, SUBLANES)
                    step = steps_ref[y, low, high, group].astype(jnp.float32)
                    new_base_ref[layer, rows, columns] = base_ref[layer, rows, columns] - step


def per_device(replica_params, outer_base, outer_momentum):
    ys, highs, lows = lax.axis_size("y"), lax.axis_size("z_hi"), lax.axis_size("z_lo")
    xs, cores = lax.axis_size("x"), lax.axis_size("core")
    replicas = ys * highs * lows
    layers, rows, width = outer_base.shape
    groups = layers * rows // SUBLANES
    limit = CLIP_RMS * math.sqrt(rows * xs * cores * width)
    params = pltpu.CompilerParams(vmem_limit_bytes=VMEM_LIMIT)
    tile = (groups, SUBLANES, BLOCK)
    vmem = pl.BlockSpec(memory_space=pltpu.VMEM)
    smem = pl.BlockSpec(memory_space=pltpu.SMEM)
    y, high, low = (lax.axis_index(name) for name in ("y", "z_hi", "z_lo"))
    place = jnp.stack([y * (highs * lows) + low, jnp.int32(lows), high]).astype(jnp.int32)

    grouped = replica_params.reshape(groups, SUBLANES, replicas, BLOCK).transpose(0, 2, 1, 3)
    blocks = pl.pallas_call(
        split_kernel,
        in_specs=[pl.BlockSpec(memory_space=pltpu.HBM)],
        out_shape=jax.ShapeDtypeStruct((ys, lows, highs, *tile), replica_params.dtype),
        scratch_shapes=[
            pltpu.VMEM((groups, replicas, SUBLANES, BLOCK), replica_params.dtype),
            pltpu.SemaphoreType.DMA((ys,)),
        ],
        compiler_params=pltpu.CompilerParams(vmem_limit_bytes=60 * 2**20),
        name="split",
    )(grouped)
    received = lax.all_to_all(
        blocks.reshape(ys * lows, highs, *tile), ("y", "z_lo"), 0, 0, tiled=True
    )
    momentum = outer_momentum.reshape(tile)

    packed = pl.pallas_call(
        partial_kernel,
        in_specs=[smem, vmem, vmem, vmem],
        out_shape=jax.ShapeDtypeStruct((highs, highs + 1, *tile), jnp.bfloat16),
        compiler_params=params,
        name="partial",
    )(place, received, outer_base, momentum)
    packed = lax.all_to_all(packed, "z_hi", 0, 0, tiled=True)

    averaged, squares = pl.pallas_call(
        lambda *refs: average_kernel(replicas, *refs),
        out_shape=(
            jax.ShapeDtypeStruct((highs, *tile), jnp.float32),
            jax.ShapeDtypeStruct((1, BLOCK), jnp.float32),
        ),
        compiler_params=params,
        name="average",
    )(packed)
    owners = ys * lows * xs
    squares = jnp.broadcast_to(lax.psum(squares, "core")[None], (owners, 1, BLOCK))
    squares = lax.all_to_all(squares, ("y", "z_lo", "x"), 0, 0, tiled=True).reshape(owners, BLOCK)

    momentum_next, step = pl.pallas_call(
        lambda *refs: step_kernel(limit, *refs),
        in_specs=[smem, vmem, vmem, vmem, vmem],
        out_shape=(
            jax.ShapeDtypeStruct(tile, jnp.float32),
            jax.ShapeDtypeStruct((ys * lows, highs, *tile), jnp.bfloat16),
        ),
        compiler_params=params,
        name="step",
    )(place, squares, averaged, packed, momentum)

    steps = lax.all_to_all(step, ("y", "z_lo"), 0, 0, tiled=True)
    chunks = 4
    new_base = pl.pallas_call(
        base_kernel,
        grid=(chunks,),
        in_specs=[
            pl.BlockSpec((ys // chunks, lows, highs, *tile), lambda i: (i, 0, 0, 0, 0, 0)),
            pl.BlockSpec((layers, rows, width // chunks), lambda i: (0, 0, i)),
        ],
        out_specs=pl.BlockSpec((layers, rows, width // chunks), lambda i: (0, 0, i)),
        out_shape=jax.ShapeDtypeStruct((layers, rows, width), jnp.float32),
        compiler_params=params,
        name="base",
    )(steps.reshape(ys, lows, highs, *tile), outer_base)
    return (new_base, momentum_next.reshape(outer_momentum.shape))


def solution(mesh):
    replicas, fsdp = mesh.devices.shape
    side = math.isqrt(replicas)
    owners, shards = ("y", "z_hi", "z_lo"), ("x", "core")
    torus = Mesh(
        mesh.devices.reshape(side, side // 2, 2, fsdp // 2, 2), owners + shards
    )
    return jax.shard_map(
        per_device,
        mesh=torus,
        in_specs=(
            P(owners, None, shards, None),
            P(None, shards, None),
            P(None, shards, owners),
        ),
        out_specs=(P(None, shards, None), P(None, shards, owners)),
        check_vma=False,
    )
```

```python
import math

import jax
import jax.numpy as jnp
from jax import lax
from jax.experimental import pallas as pl
from jax.experimental.pallas import tpu as pltpu
from jax.sharding import Mesh, PartitionSpec as P

BLOCK = 128


CODE_RANGE = 448.0
EPSILON = 1e-06
OUTER_RATE = 0.7
NESTEROV = 0.9
CLIP_RMS = 0.001
SUBLANES = 8
VMEM_LIMIT = 8 * 2**20


def split_kernel(params_ref, blocks_ref, held_ref, moved_ref, in_semaphores, out_semaphores):
    ys, lows, highs = blocks_ref.shape[:3]
    share = highs * lows
    reads = [
        pltpu.make_async_copy(
            params_ref.at[:, pl.ds(y * share, share)], held_ref.at[y], in_semaphores.at[y]
        )
        for y in range(ys)
    ]
    writes = [
        pltpu.make_async_copy(moved_ref.at[y], blocks_ref.at[y], out_semaphores.at[y])
        for y in range(ys)
    ]
    for read in reads:
        read.start()
    for y in range(ys):
        reads[y].wait()
        for low in range(lows):
            for high in range(highs):
                moved_ref[y, low, high] = held_ref[y, :, high * lows + low]
        writes[y].start()
    for write in writes:
        write.wait()


def partial_kernel(received_ref, base_ref, momentum_ref, packed_ref):
    sources, blocks, groups = received_ref.shape[:3]
    peers = packed_ref.shape[0]
    lows = lax.axis_size("z_lo")
    first = lax.axis_index("y") * (blocks * lows) + lax.axis_index("z_lo")
    for block in range(blocks):
        start = pl.multiple_of((first + block * lows) * BLOCK, BLOCK)
        base = base_ref[:, :, pl.ds(start, BLOCK)].reshape(groups, SUBLANES, BLOCK)
        summed = jnp.zeros(base.shape, jnp.float32)
        for source in range(sources):
            difference = base - received_ref[source, block].astype(jnp.float32)
            largest = jnp.max(jnp.abs(difference), axis=-1, keepdims=True)
            scales = ((largest + EPSILON) / CODE_RANGE).astype(jnp.bfloat16).astype(jnp.float32)
            code_words = (difference / scales).astype(jnp.bfloat16)
            summed = summed + code_words.astype(jnp.float32) * scales
        sent = summed.astype(jnp.bfloat16)
        for peer in range(peers):
            packed_ref[peer, block] = sent
    momentum = momentum_ref[...].astype(jnp.bfloat16)
    for peer in range(peers):
        packed_ref[peer, blocks] = momentum


def average_kernel(replicas, packed_ref, averaged_ref, square_ref):
    sources = packed_ref.shape[0]
    blocks, groups = averaged_ref.shape[:2]
    squares = jnp.zeros((groups, SUBLANES, BLOCK), jnp.float32)
    for block in range(blocks):
        summed = packed_ref[0, block].astype(jnp.float32)
        for source in range(1, sources):
            summed = summed + packed_ref[source, block].astype(jnp.float32)
        averaged = summed / replicas
        averaged_ref[block] = averaged
        squares = squares + averaged * averaged
    half = groups // 2
    first = jnp.sum(jnp.sum(jnp.sum(squares[:half], axis=0), axis=0, keepdims=True), axis=-1, keepdims=True)
    second = jnp.sum(jnp.sum(jnp.sum(squares[half:], axis=0), axis=0, keepdims=True), axis=-1, keepdims=True)
    lanes = lax.broadcasted_iota(jnp.int32, square_ref.shape, 1)
    square_ref[...] = jnp.where(lanes < BLOCK // 2, first, second)


def step_kernel(limit, squares_ref, averaged_ref, packed_ref, momentum_ref, momentum_next_ref, step_ref):
    blocks, groups = averaged_ref.shape[:2]
    sums = jnp.sum(squares_ref[...], axis=0, keepdims=True)
    mine = lax.axis_index("z_hi")
    for group in range(groups):
        layer = group * 2 // groups
        total = jnp.max(sums[:, layer * 64 : (layer + 1) * 64], axis=-1, keepdims=True)
        factor = jnp.minimum(1.0, limit / (jnp.sqrt(total) + EPSILON))
        momentum_next_ref[group] = NESTEROV * momentum_ref[group] + averaged_ref[mine, group] * factor
        for block in range(blocks):
            clipped = averaged_ref[block, group] * factor
            momentum_next = NESTEROV * packed_ref[block, blocks, group].astype(jnp.float32) + clipped
            step = (OUTER_RATE * (clipped + NESTEROV * momentum_next)).astype(jnp.bfloat16)
            for target in range(step_ref.shape[0]):
                step_ref[target, block, group] = step


def base_kernel(steps_ref, base_ref, new_base_ref, made_ref, semaphores):
    ys, lows, highs, groups = steps_ref.shape[:4]
    layers = base_ref.shape[0]
    chunks = semaphores.shape[0]
    chunk = base_ref.shape[2] // chunks
    writes = []
    for part in range(chunks):
        for y in range(part * ys // chunks, (part + 1) * ys // chunks):
            for high in range(highs):
                for low in range(lows):
                    columns = pl.ds(((y * highs + high) * lows + low) * BLOCK, BLOCK)
                    for group in range(groups):
                        layer, half = divmod(group, groups // layers)
                        rows = pl.ds(half * SUBLANES, SUBLANES)
                        step = steps_ref[y, low, high, group].astype(jnp.float32)
                        made_ref[layer, rows, columns] = base_ref[layer, rows, columns] - step
        columns = pl.ds(part * chunk, chunk)
        write = pltpu.make_async_copy(
            made_ref.at[:, :, columns], new_base_ref.at[:, :, columns], semaphores.at[part]
        )
        write.start()
        writes.append(write)
    for write in writes:
        write.wait()


def per_device(replica_params, outer_base, outer_momentum):
    ys, highs, lows = lax.axis_size("y"), lax.axis_size("z_hi"), lax.axis_size("z_lo")
    xs, cores = lax.axis_size("x"), lax.axis_size("core")
    replicas = ys * highs * lows
    layers, rows, width = outer_base.shape
    groups = layers * rows // SUBLANES
    limit = CLIP_RMS * math.sqrt(rows * xs * cores * width)
    params = pltpu.CompilerParams(vmem_limit_bytes=VMEM_LIMIT)
    tile = (groups, SUBLANES, BLOCK)
    vmem = pl.BlockSpec(memory_space=pltpu.VMEM)
    grouped = replica_params.reshape(groups, SUBLANES, replicas, BLOCK).transpose(0, 2, 1, 3)
    anywhere = pl.BlockSpec(memory_space=pl.ANY)
    blocks = pl.pallas_call(
        split_kernel,
        in_specs=[anywhere],
        out_specs=anywhere,
        out_shape=jax.ShapeDtypeStruct((ys, lows, highs, *tile), replica_params.dtype),
        scratch_shapes=[
            pltpu.VMEM((ys, groups, highs * lows, SUBLANES, BLOCK), replica_params.dtype),
            pltpu.VMEM((ys, lows, highs, *tile), replica_params.dtype),
            pltpu.SemaphoreType.DMA((ys,)),
            pltpu.SemaphoreType.DMA((ys,)),
        ],
        compiler_params=pltpu.CompilerParams(vmem_limit_bytes=60 * 2**20),
        name="split",
    )(grouped)
    blocks, outer_base = lax.optimization_barrier((blocks, outer_base))
    received = lax.all_to_all(
        blocks.reshape(ys * lows, highs, *tile), ("y", "z_lo"), 0, 0, tiled=True
    )
    momentum = outer_momentum.reshape(tile)

    packed = pl.pallas_call(
        partial_kernel,
        out_shape=jax.ShapeDtypeStruct((highs, highs + 1, *tile), jnp.bfloat16),
        compiler_params=params,
        name="partial",
    )(received, outer_base, momentum)
    packed = lax.all_to_all(packed, "z_hi", 0, 0, tiled=True)

    averaged, squares = pl.pallas_call(
        lambda *refs: average_kernel(replicas, *refs),
        out_shape=(
            jax.ShapeDtypeStruct((highs, *tile), jnp.float32),
            jax.ShapeDtypeStruct((1, BLOCK), jnp.float32),
        ),
        compiler_params=params,
        name="average",
    )(packed)
    owners = ys * lows * xs
    squares = jnp.broadcast_to(lax.psum(squares, "core")[None], (owners, 1, BLOCK))
    squares = lax.all_to_all(squares, ("y", "z_lo", "x"), 0, 0, tiled=True).reshape(owners, BLOCK)

    momentum_next, step = pl.pallas_call(
        lambda *refs: step_kernel(limit, *refs),
        out_shape=(
            jax.ShapeDtypeStruct(tile, jnp.float32),
            jax.ShapeDtypeStruct((ys * lows, highs, *tile), jnp.bfloat16),
        ),
        compiler_params=params,
        name="step",
    )(squares, averaged, packed, momentum)

    steps = lax.all_to_all(step, ("y", "z_lo"), 0, 0, tiled=True)
    chunks = 4
    new_base = pl.pallas_call(
        base_kernel,
        in_specs=[vmem, vmem],
        out_specs=anywhere,
        out_shape=jax.ShapeDtypeStruct((layers, rows, width), jnp.float32),
        scratch_shapes=[
            pltpu.VMEM((layers, rows, width), jnp.float32),
            pltpu.SemaphoreType.DMA((chunks,)),
        ],
        compiler_params=params,
        name="base",
    )(steps.reshape(ys, lows, highs, *tile), outer_base)
    return (new_base, momentum_next.reshape(outer_momentum.shape))


def solution(mesh):
    replicas, fsdp = mesh.devices.shape
    side = math.isqrt(replicas)
    owners, shards = ("y", "z_hi", "z_lo"), ("x", "core")
    torus = Mesh(
        mesh.devices.reshape(side, side // 2, 2, fsdp // 2, 2), owners + shards
    )
    return jax.shard_map(
        per_device,
        mesh=torus,
        in_specs=(
            P(owners, None, shards, None),
            P(None, shards, None),
            P(None, shards, owners),
        ),
        out_specs=(P(None, shards, None), P(None, shards, owners)),
        check_vma=False,
    )
```

```python
import math

import jax
import jax.numpy as jnp
from jax import lax
from jax.experimental import pallas as pl
from jax.experimental.pallas import tpu as pltpu
from jax.sharding import Mesh, PartitionSpec as P

BLOCK = 128


CODE_RANGE = 448.0
EPSILON = 1e-06
OUTER_RATE = 0.7
NESTEROV = 0.9
CLIP_RMS = 0.001
SUBLANES = 8
VMEM_LIMIT = 8 * 2**20


def split_kernel(params_ref, blocks_ref):
    ys, lows, highs = blocks_ref.shape[:3]
    for y in range(ys):
        for low in range(lows):
            for high in range(highs):
                blocks_ref[y, low, high] = params_ref[:, (y * highs + high) * lows + low]


def partial_kernel(received_ref, base_ref, momentum_ref, packed_ref):
    sources, blocks, groups = received_ref.shape[:3]
    peers = packed_ref.shape[0]
    lows = lax.axis_size("z_lo")
    first = lax.axis_index("y") * (blocks * lows) + lax.axis_index("z_lo")
    for block in range(blocks):
        start = pl.multiple_of((first + block * lows) * BLOCK, BLOCK)
        base = base_ref[:, :, pl.ds(start, BLOCK)].reshape(groups, SUBLANES, BLOCK)
        summed = jnp.zeros(base.shape, jnp.float32)
        for source in range(sources):
            difference = base - received_ref[source, block].astype(jnp.float32)
            largest = jnp.max(jnp.abs(difference), axis=-1, keepdims=True)
            scales = ((largest + EPSILON) / CODE_RANGE).astype(jnp.bfloat16).astype(jnp.float32)
            code_words = (difference / scales).astype(jnp.bfloat16)
            summed = summed + code_words.astype(jnp.float32) * scales
        sent = summed.astype(jnp.bfloat16)
        for peer in range(peers):
            packed_ref[peer, block] = sent
    momentum = momentum_ref[...].astype(jnp.bfloat16)
    for peer in range(peers):
        packed_ref[peer, blocks] = momentum


def average_kernel(replicas, packed_ref, averaged_ref, square_ref):
    sources, cores = packed_ref.shape[:2]
    blocks, groups = averaged_ref.shape[:2]

    def average(core, block):
        summed = packed_ref[0, core, block].astype(jnp.float32)
        for source in range(1, sources):
            summed = summed + packed_ref[source, core, block].astype(jnp.float32)
        return summed / replicas

    squares = jnp.zeros((groups, SUBLANES, BLOCK), jnp.float32)
    for block in range(blocks):
        averaged_ref[block] = average(lax.axis_index("core"), block)
        for core in range(cores):
            averaged = average(core, block)
            squares = squares + averaged * averaged
    half = groups // 2
    first = jnp.sum(jnp.sum(jnp.sum(squares[:half], axis=0), axis=0, keepdims=True), axis=-1, keepdims=True)
    second = jnp.sum(jnp.sum(jnp.sum(squares[half:], axis=0), axis=0, keepdims=True), axis=-1, keepdims=True)
    lanes = lax.broadcasted_iota(jnp.int32, square_ref.shape, 1)
    square_ref[...] = jnp.where(lanes < BLOCK // 2, first, second)


def step_kernel(limit, squares_ref, averaged_ref, packed_ref, momentum_ref, momentum_next_ref, step_ref):
    blocks, groups = averaged_ref.shape[:2]
    sums = jnp.sum(squares_ref[...], axis=0, keepdims=True)
    mine, core = lax.axis_index("z_hi"), lax.axis_index("core")
    for group in range(groups):
        layer = group * 2 // groups
        total = jnp.max(sums[:, layer * 64 : (layer + 1) * 64], axis=-1, keepdims=True)
        factor = jnp.minimum(1.0, limit / (jnp.sqrt(total) + EPSILON))
        momentum_next_ref[group] = NESTEROV * momentum_ref[group] + averaged_ref[mine, group] * factor
        for block in range(blocks):
            clipped = averaged_ref[block, group] * factor
            momentum_next = NESTEROV * packed_ref[block, core, blocks, group].astype(jnp.float32) + clipped
            step = (OUTER_RATE * (clipped + NESTEROV * momentum_next)).astype(jnp.bfloat16)
            for target in range(step_ref.shape[0]):
                step_ref[target, block, group] = step


def base_kernel(steps_ref, base_ref, new_base_ref, made_ref, semaphores):
    ys, lows, highs, groups = steps_ref.shape[:4]
    layers = base_ref.shape[0]
    chunks = semaphores.shape[0]
    chunk = base_ref.shape[2] // chunks
    writes = []
    for part in range(chunks):
        for y in range(part * ys // chunks, (part + 1) * ys // chunks):
            for high in range(highs):
                for low in range(lows):
                    columns = pl.ds(((y * highs + high) * lows + low) * BLOCK, BLOCK)
                    for group in range(groups):
                        layer, half = divmod(group, groups // layers)
                        rows = pl.ds(half * SUBLANES, SUBLANES)
                        step = steps_ref[y, low, high, group].astype(jnp.float32)
                        made_ref[layer, rows, columns] = base_ref[layer, rows, columns] - step
        columns = pl.ds(part * chunk, chunk)
        write = pltpu.make_async_copy(
            made_ref.at[:, :, columns], new_base_ref.at[:, :, columns], semaphores.at[part]
        )
        write.start()
        writes.append(write)
    for write in writes:
        write.wait()


def per_device(replica_params, outer_base, outer_momentum):
    ys, highs, lows = lax.axis_size("y"), lax.axis_size("z_hi"), lax.axis_size("z_lo")
    xs, cores = lax.axis_size("x"), lax.axis_size("core")
    replicas = ys * highs * lows
    layers, rows, width = outer_base.shape
    groups = layers * rows // SUBLANES
    limit = CLIP_RMS * math.sqrt(rows * xs * cores * width)
    params = pltpu.CompilerParams(vmem_limit_bytes=VMEM_LIMIT)
    tile = (groups, SUBLANES, BLOCK)
    vmem = pl.BlockSpec(memory_space=pltpu.VMEM)
    grouped = replica_params.reshape(groups, SUBLANES, replicas, BLOCK).transpose(0, 2, 1, 3)
    blocks = pl.pallas_call(
        split_kernel,
        out_shape=jax.ShapeDtypeStruct((ys, lows, highs, *tile), replica_params.dtype),
        compiler_params=params,
        name="split",
    )(grouped)
    received = lax.all_to_all(
        blocks.reshape(ys * lows, highs, *tile), ("y", "z_lo"), 0, 0, tiled=True
    )
    momentum = outer_momentum.reshape(tile)

    packed = pl.pallas_call(
        partial_kernel,
        out_shape=jax.ShapeDtypeStruct((highs * cores, highs + 1, *tile), jnp.bfloat16),
        compiler_params=params,
        name="partial",
    )(received, outer_base, momentum)
    packed = lax.all_to_all(packed, ("z_hi", "core"), 0, 0, tiled=True)
    packed = packed.reshape(highs, cores, highs + 1, *tile)

    owners = ys * lows * xs
    averaged, squares = pl.pallas_call(
        lambda *refs: average_kernel(replicas, *refs),
        out_shape=(
            jax.ShapeDtypeStruct((highs, *tile), jnp.float32),
            jax.ShapeDtypeStruct((owners, BLOCK), jnp.float32),
        ),
        compiler_params=params,
        name="average",
    )(packed)
    squares = lax.all_to_all(
        squares.reshape(owners, 1, BLOCK), ("y", "z_lo", "x"), 0, 0, tiled=True
    ).reshape(owners, BLOCK)

    momentum_next, step = pl.pallas_call(
        lambda *refs: step_kernel(limit, *refs),
        out_shape=(
            jax.ShapeDtypeStruct(tile, jnp.float32),
            jax.ShapeDtypeStruct((ys * lows, highs, *tile), jnp.bfloat16),
        ),
        compiler_params=params,
        name="step",
    )(squares, averaged, packed, momentum)

    steps = lax.all_to_all(step, ("y", "z_lo"), 0, 0, tiled=True)
    chunks = 4
    new_base = pl.pallas_call(
        base_kernel,
        in_specs=[vmem, vmem],
        out_specs=pl.BlockSpec(memory_space=pl.ANY),
        out_shape=jax.ShapeDtypeStruct((layers, rows, width), jnp.float32),
        scratch_shapes=[
            pltpu.VMEM((layers, rows, width), jnp.float32),
            pltpu.SemaphoreType.DMA((chunks,)),
        ],
        compiler_params=params,
        name="base",
    )(steps.reshape(ys, lows, highs, *tile), outer_base)
    return (new_base, momentum_next.reshape(outer_momentum.shape))


def solution(mesh):
    replicas, fsdp = mesh.devices.shape
    side = math.isqrt(replicas)
    owners, shards = ("y", "z_hi", "z_lo"), ("x", "core")
    torus = Mesh(
        mesh.devices.reshape(side, side // 2, 2, fsdp // 2, 2), owners + shards
    )
    return jax.shard_map(
        per_device,
        mesh=torus,
        in_specs=(
            P(owners, None, shards, None),
            P(None, shards, None),
            P(None, shards, owners),
        ),
        out_specs=(P(None, shards, None), P(None, shards, owners)),
        check_vma=False,
    )
```

```python
import math

import jax
import jax.numpy as jnp
from jax import lax
from jax.experimental import pallas as pl
from jax.experimental.pallas import tpu as pltpu
from jax.sharding import Mesh, PartitionSpec as P

BLOCK = 128


CODE_RANGE = 448.0
EPSILON = 1e-06
OUTER_RATE = 0.7
NESTEROV = 0.9
CLIP_RMS = 0.001
SUBLANES = 8
VMEM_LIMIT = 8 * 2**20


def split_kernel(params_ref, momentum_ref, blocks_ref):
    ys, lows, entries = blocks_ref.shape[:3]
    highs = entries - 1
    momentum = momentum_ref[...].astype(jnp.bfloat16)
    for y in range(ys):
        for low in range(lows):
            for high in range(highs):
                blocks_ref[y, low, high] = params_ref[:, (y * highs + high) * lows + low]
            blocks_ref[y, low, highs] = momentum


def partial_kernel(received_ref, base_ref, packed_ref):
    sources = received_ref.shape[0]
    peers, blocks, groups = packed_ref.shape[:3]
    lows = lax.axis_size("z_lo")
    first = lax.axis_index("y") * (blocks * lows) + lax.axis_index("z_lo")
    for block in range(blocks):
        start = pl.multiple_of((first + block * lows) * BLOCK, BLOCK)
        base = base_ref[:, :, pl.ds(start, BLOCK)].reshape(groups, SUBLANES, BLOCK)
        summed = jnp.zeros(base.shape, jnp.float32)
        for source in range(sources):
            difference = base - received_ref[source, block].astype(jnp.float32)
            largest = jnp.max(jnp.abs(difference), axis=-1, keepdims=True)
            scales = ((largest + EPSILON) / CODE_RANGE).astype(jnp.bfloat16).astype(jnp.float32)
            code_words = (difference / scales).astype(jnp.bfloat16)
            summed = summed + code_words.astype(jnp.float32) * scales
        sent = summed.astype(jnp.bfloat16)
        for peer in range(peers):
            packed_ref[peer, block] = sent


def average_kernel(replicas, packed_ref, received_ref, averaged_ref, sent_ref, momenta_ref):
    sources, blocks, groups = packed_ref.shape[:3]
    peers = sent_ref.shape[0]

    def average(block):
        summed = packed_ref[0, block].astype(jnp.float32)
        for source in range(1, sources):
            summed = summed + packed_ref[source, block].astype(jnp.float32)
        return summed / replicas

    averaged_ref[...] = average(lax.axis_index("z_hi"))
    squares = jnp.zeros((groups, SUBLANES, BLOCK), jnp.float32)
    for block in range(blocks):
        averaged = average(block)
        squares = squares + averaged * averaged
        sent = averaged.astype(jnp.bfloat16)
        for peer in range(peers):
            sent_ref[peer, block * groups : (block + 1) * groups] = sent
    half = groups // 2
    first = jnp.sum(jnp.sum(jnp.sum(squares[:half], axis=0), axis=0, keepdims=True), axis=-1, keepdims=True)
    second = jnp.sum(jnp.sum(jnp.sum(squares[half:], axis=0), axis=0, keepdims=True), axis=-1, keepdims=True)
    tile = (SUBLANES, BLOCK)
    lanes = lax.broadcasted_iota(jnp.int32, tile, 1)
    rows = lax.broadcasted_iota(jnp.int32, tile, 0)
    rest = jnp.where(lanes < BLOCK // 2, first, second)
    pieces = jnp.zeros(tile, jnp.float32)
    for piece in range(3):
        rounded = rest.astype(jnp.bfloat16).astype(jnp.float32)
        pieces = jnp.where(rows == piece, rounded, pieces)
        rest = rest - rounded
    pieces = pieces.astype(jnp.bfloat16)
    for peer in range(peers):
        sent_ref[peer, blocks * groups] = pieces
        momenta_ref[peer] = received_ref[peer, blocks]


def sum_kernel(sent_ref, sums_ref):
    sources, tiles = sent_ref.shape[:2]
    total = sent_ref[0, tiles - 1].astype(jnp.float32)
    for source in range(1, sources):
        total = total + sent_ref[source, tiles - 1].astype(jnp.float32)
    sums_ref[...] = jnp.broadcast_to(jnp.sum(total, axis=0, keepdims=True), sums_ref.shape)


def base_kernel(limit, sums_ref, sent_ref, base_ref, averaged_ref, momentum_ref, *refs):
    *momenta_refs, new_base_ref, momentum_next_ref, made_ref, semaphores = refs
    highs = len(momenta_refs)
    groups = averaged_ref.shape[0]
    layers, _, width = base_ref.shape
    lows = lax.axis_size("z_lo")
    ys = sent_ref.shape[0] // lows
    sums = jnp.sum(sums_ref[...], axis=0, keepdims=True)
    factors = []
    for layer in range(layers):
        share = BLOCK // layers
        total = jnp.max(sums[:, layer * share : (layer + 1) * share], axis=-1, keepdims=True)
        factors.append(jnp.minimum(1.0, limit / (jnp.sqrt(total) + EPSILON)))
    for group in range(groups):
        factor = factors[group * layers // groups]
        momentum_next_ref[group] = NESTEROV * momentum_ref[group] + averaged_ref[group] * factor
    chunks = semaphores.shape[0]
    chunk = width // chunks
    mine = lax.axis_index("z_hi")
    writes = []
    for part in range(chunks):
        for y in range(part * ys // chunks, (part + 1) * ys // chunks):
            for shift in range(highs):
                high = lax.rem(mine + shift, highs)
                for low in range(lows):
                    start = pl.multiple_of(((y * highs + high) * lows + low) * BLOCK, BLOCK)
                    columns = pl.ds(start, BLOCK)
                    source = y * lows + low
                    for group in range(groups):
                        layer, half = divmod(group, groups // layers)
                        rows = pl.ds(half * SUBLANES, SUBLANES)
                        averaged = sent_ref[source, high * groups + group].astype(jnp.float32)
                        clipped = averaged * factors[layer]
                        momentum = momenta_refs[shift][source, group].astype(jnp.float32)
                        momentum_next = NESTEROV * momentum + clipped
                        step = (OUTER_RATE * (clipped + NESTEROV * momentum_next)).astype(jnp.bfloat16)
                        made_ref[layer, rows, columns] = (
                            base_ref[layer, rows, columns] - step.astype(jnp.float32)
                        )
        columns = pl.ds(part * chunk, chunk)
        write = pltpu.make_async_copy(
            made_ref.at[:, :, columns], new_base_ref.at[:, :, columns], semaphores.at[part]
        )
        write.start()
        writes.append(write)
    for write in writes:
        write.wait()


def per_device(replica_params, outer_base, outer_momentum):
    ys, highs, lows = lax.axis_size("y"), lax.axis_size("z_hi"), lax.axis_size("z_lo")
    xs, cores = lax.axis_size("x"), lax.axis_size("core")
    replicas = ys * highs * lows
    layers, rows, width = outer_base.shape
    groups = layers * rows // SUBLANES
    limit = CLIP_RMS * math.sqrt(rows * xs * cores * width)
    params = pltpu.CompilerParams(vmem_limit_bytes=VMEM_LIMIT)
    tile = (groups, SUBLANES, BLOCK)
    owners = ys * lows
    momentum = outer_momentum.reshape(tile)

    grouped = replica_params.reshape(groups, SUBLANES, replicas, BLOCK).transpose(0, 2, 1, 3)
    blocks = pl.pallas_call(
        split_kernel,
        out_shape=jax.ShapeDtypeStruct((ys, lows, highs + 1, *tile), replica_params.dtype),
        compiler_params=params,
        name="split",
    )(grouped, momentum)
    received = lax.all_to_all(
        blocks.reshape(owners, highs + 1, *tile), ("y", "z_lo"), 0, 0, tiled=True
    )
    packed = pl.pallas_call(
        partial_kernel,
        out_shape=jax.ShapeDtypeStruct((highs, highs, *tile), jnp.bfloat16),
        compiler_params=params,
        name="partial",
    )(received, outer_base)
    packed = lax.all_to_all(packed, "z_hi", 0, 0, tiled=True)

    averaged, sent, momenta = pl.pallas_call(
        lambda *refs: average_kernel(replicas, *refs),
        out_shape=(
            jax.ShapeDtypeStruct(tile, jnp.float32),
            jax.ShapeDtypeStruct((owners, highs * groups + 1, SUBLANES, BLOCK), jnp.bfloat16),
            jax.ShapeDtypeStruct((owners, *tile), jnp.bfloat16),
        ),
        compiler_params=params,
        name="average",
    )(packed, received)
    sent = lax.all_to_all(sent, ("y", "z_lo"), 0, 0, tiled=True)
    all_momenta = [momenta] + [
        lax.ppermute(momenta, "z_hi", [(i, (i - shift) % highs) for i in range(highs)])
        for shift in range(1, highs)
    ]
    shards = xs * cores
    sums = pl.pallas_call(
        sum_kernel,
        out_shape=jax.ShapeDtypeStruct((shards, BLOCK), jnp.float32),
        compiler_params=params,
        name="sum",
    )(sent)
    sums = lax.all_to_all(
        sums.reshape(shards, 1, BLOCK), ("x", "core"), 0, 0, tiled=True
    ).reshape(shards, BLOCK)

    chunks = 4
    vmem = pl.BlockSpec(memory_space=pltpu.VMEM)
    new_base, momentum_next = pl.pallas_call(
        lambda *refs: base_kernel(limit, *refs),
        in_specs=[vmem] * (5 + highs),
        out_specs=(pl.BlockSpec(memory_space=pl.ANY), vmem),
        out_shape=(
            jax.ShapeDtypeStruct((layers, rows, width), jnp.float32),
            jax.ShapeDtypeStruct(tile, jnp.float32),
        ),
        scratch_shapes=[
            pltpu.VMEM((layers, rows, width), jnp.float32),
            pltpu.SemaphoreType.DMA((chunks,)),
        ],
        compiler_params=params,
        name="base",
    )(sums, sent, outer_base, averaged, momentum, *all_momenta)
    return (new_base, momentum_next.reshape(outer_momentum.shape))


def solution(mesh):
    replicas, fsdp = mesh.devices.shape
    side = math.isqrt(replicas)
    owners, shards = ("y", "z_hi", "z_lo"), ("x", "core")
    torus = Mesh(
        mesh.devices.reshape(side, side // 2, 2, fsdp // 2, 2), owners + shards
    )
    return jax.shard_map(
        per_device,
        mesh=torus,
        in_specs=(
            P(owners, None, shards, None),
            P(None, shards, None),
            P(None, shards, owners),
        ),
        out_specs=(P(None, shards, None), P(None, shards, owners)),
        check_vma=False,
    )
```

```python
import math

import jax
import jax.numpy as jnp
from jax import lax
from jax.experimental import pallas as pl
from jax.experimental.pallas import tpu as pltpu
from jax.sharding import Mesh, PartitionSpec as P

BLOCK = 128


CODE_RANGE = 448.0
EPSILON = 1e-06
OUTER_RATE = 0.7
NESTEROV = 0.9
CLIP_RMS = 0.001
SUBLANES = 8
VMEM_LIMIT = 8 * 2**20


def split_kernel(params_ref, momentum_ref, blocks_ref):
    ys, lows, entries = blocks_ref.shape[:3]
    highs = entries - 1
    momentum = momentum_ref[...]
    for y in range(ys):
        for low in range(lows):
            for high in range(highs):
                blocks_ref[y, low, high] = params_ref[:, (y * highs + high) * lows + low]
            blocks_ref[y, low, highs] = momentum


def partial_kernel(received_ref, base_ref, packed_ref):
    sources = received_ref.shape[0]
    peers, blocks, groups = packed_ref.shape[:3]
    lows = lax.axis_size("z_lo")
    first = lax.axis_index("y") * (blocks * lows) + lax.axis_index("z_lo")
    for block in range(blocks):
        start = pl.multiple_of((first + block * lows) * BLOCK, BLOCK)
        base = base_ref[:, :, pl.ds(start, BLOCK)].reshape(groups, SUBLANES, BLOCK)
        summed = jnp.zeros(base.shape, jnp.float32)
        for source in range(sources):
            difference = base - received_ref[source, block].astype(jnp.float32)
            largest = jnp.max(jnp.abs(difference), axis=-1, keepdims=True)
            scales = ((largest + EPSILON) / CODE_RANGE).astype(jnp.bfloat16).astype(jnp.float32)
            code_words = (difference / scales).astype(jnp.bfloat16)
            summed = summed + code_words.astype(jnp.float32) * scales
        sent = summed.astype(jnp.bfloat16)
        for peer in range(peers):
            packed_ref[peer, block] = sent


def average_kernel(replicas, packed_ref, received_ref, averaged_ref, sent_ref, momenta_ref):
    sources, blocks, groups = packed_ref.shape[:3]
    peers = sent_ref.shape[0]

    def average(block):
        summed = packed_ref[0, block].astype(jnp.float32)
        for source in range(1, sources):
            summed = summed + packed_ref[source, block].astype(jnp.float32)
        return summed / replicas

    averaged_ref[...] = average(lax.axis_index("z_hi"))
    squares = jnp.zeros((groups, SUBLANES, BLOCK), jnp.float32)
    for block in range(blocks):
        averaged = average(block)
        squares = squares + averaged * averaged
        sent = averaged.astype(jnp.bfloat16)
        for peer in range(peers):
            sent_ref[peer, block * groups : (block + 1) * groups] = sent
    half = groups // 2
    first = jnp.sum(jnp.sum(jnp.sum(squares[:half], axis=0), axis=0, keepdims=True), axis=-1, keepdims=True)
    second = jnp.sum(jnp.sum(jnp.sum(squares[half:], axis=0), axis=0, keepdims=True), axis=-1, keepdims=True)
    tile = (SUBLANES, BLOCK)
    lanes = lax.broadcasted_iota(jnp.int32, tile, 1)
    rows = lax.broadcasted_iota(jnp.int32, tile, 0)
    rest = jnp.where(lanes < BLOCK // 2, first, second)
    pieces = jnp.zeros(tile, jnp.float32)
    for piece in range(3):
        rounded = rest.astype(jnp.bfloat16).astype(jnp.float32)
        pieces = jnp.where(rows == piece, rounded, pieces)
        rest = rest - rounded
    pieces = pieces.astype(jnp.bfloat16)
    for peer in range(peers):
        sent_ref[peer, blocks * groups] = pieces
        momenta_ref[peer] = received_ref[peer, blocks]


def sum_kernel(sent_ref, sums_ref):
    sources, tiles = sent_ref.shape[:2]
    total = sent_ref[0, tiles - 1].astype(jnp.float32)
    for source in range(1, sources):
        total = total + sent_ref[source, tiles - 1].astype(jnp.float32)
    sums_ref[...] = jnp.broadcast_to(jnp.sum(total, axis=0, keepdims=True), sums_ref.shape)


def base_kernel(limit, sums_ref, sent_ref, base_ref, averaged_ref, momentum_ref, *refs):
    *momenta_refs, new_base_ref, momentum_next_ref, made_ref, semaphores = refs
    highs = len(momenta_refs)
    groups = averaged_ref.shape[0]
    layers, _, width = base_ref.shape
    lows = lax.axis_size("z_lo")
    ys = sent_ref.shape[0] // lows
    sums = jnp.sum(sums_ref[...], axis=0, keepdims=True)
    factors = []
    for layer in range(layers):
        share = BLOCK // layers
        total = jnp.max(sums[:, layer * share : (layer + 1) * share], axis=-1, keepdims=True)
        factors.append(jnp.minimum(1.0, limit / (jnp.sqrt(total) + EPSILON)))
    rates = [OUTER_RATE * (1.0 + NESTEROV) * factor for factor in factors]
    momentum_rate = OUTER_RATE * NESTEROV * NESTEROV
    chunks = semaphores.shape[0]
    chunk = width // chunks
    mine = lax.axis_index("z_hi")
    writes = []
    for part in range(chunks):
        for y in range(part * ys // chunks, (part + 1) * ys // chunks):
            for shift in range(highs):
                high = lax.rem(mine + shift, highs)
                for low in range(lows):
                    start = pl.multiple_of(((y * highs + high) * lows + low) * BLOCK, BLOCK)
                    columns = pl.ds(start, BLOCK)
                    source = y * lows + low
                    for group in range(groups):
                        layer, half = divmod(group, groups // layers)
                        rows = pl.ds(half * SUBLANES, SUBLANES)
                        averaged = sent_ref[source, high * groups + group].astype(jnp.float32)
                        momentum = momenta_refs[shift][source, group].astype(jnp.float32)
                        step = (averaged * rates[layer] + momentum * momentum_rate).astype(jnp.bfloat16)
                        made_ref[layer, rows, columns] = (
                            base_ref[layer, rows, columns] - step.astype(jnp.float32)
                        )
        columns = pl.ds(part * chunk, chunk)
        write = pltpu.make_async_copy(
            made_ref.at[:, :, columns], new_base_ref.at[:, :, columns], semaphores.at[part]
        )
        write.start()
        writes.append(write)
    for group in range(groups):
        factor = factors[group * layers // groups]
        momentum_next_ref[group] = NESTEROV * momentum_ref[group] + averaged_ref[group] * factor
    for write in writes:
        write.wait()


def per_device(replica_params, outer_base, outer_momentum):
    ys, highs, lows = lax.axis_size("y"), lax.axis_size("z_hi"), lax.axis_size("z_lo")
    xs, cores = lax.axis_size("x"), lax.axis_size("core")
    replicas = ys * highs * lows
    layers, rows, width = outer_base.shape
    groups = layers * rows // SUBLANES
    limit = CLIP_RMS * math.sqrt(rows * xs * cores * width)
    params = pltpu.CompilerParams(vmem_limit_bytes=VMEM_LIMIT)
    tile = (groups, SUBLANES, BLOCK)
    owners = ys * lows
    momentum = outer_momentum.reshape(tile)

    grouped = replica_params.reshape(groups, SUBLANES, replicas, BLOCK).transpose(0, 2, 1, 3)
    blocks = pl.pallas_call(
        split_kernel,
        out_shape=jax.ShapeDtypeStruct((ys, lows, highs + 1, *tile), replica_params.dtype),
        compiler_params=params,
        name="split",
    )(grouped, momentum.astype(jnp.bfloat16))
    received = lax.all_to_all(
        blocks.reshape(owners, highs + 1, *tile), ("y", "z_lo"), 0, 0, tiled=True
    )
    packed = pl.pallas_call(
        partial_kernel,
        out_shape=jax.ShapeDtypeStruct((highs, highs, *tile), jnp.bfloat16),
        compiler_params=params,
        name="partial",
    )(received, outer_base)
    packed = lax.all_to_all(packed, "z_hi", 0, 0, tiled=True)

    averaged, sent, momenta = pl.pallas_call(
        lambda *refs: average_kernel(replicas, *refs),
        out_shape=(
            jax.ShapeDtypeStruct(tile, jnp.float32),
            jax.ShapeDtypeStruct((owners, highs * groups + 1, SUBLANES, BLOCK), jnp.bfloat16),
            jax.ShapeDtypeStruct((owners, *tile), jnp.bfloat16),
        ),
        compiler_params=params,
        name="average",
    )(packed, received)
    sent = lax.all_to_all(sent, ("y", "z_lo"), 0, 0, tiled=True)
    all_momenta = [momenta] + [
        lax.ppermute(momenta, "z_hi", [(i, (i - shift) % highs) for i in range(highs)])
        for shift in range(1, highs)
    ]
    shards = xs * cores
    sums = pl.pallas_call(
        sum_kernel,
        out_shape=jax.ShapeDtypeStruct((shards, BLOCK), jnp.float32),
        compiler_params=params,
        name="sum",
    )(sent)
    sums = lax.all_to_all(
        sums.reshape(shards, 1, BLOCK), ("x", "core"), 0, 0, tiled=True
    ).reshape(shards, BLOCK)

    chunks = 8
    vmem = pl.BlockSpec(memory_space=pltpu.VMEM)
    new_base, momentum_next = pl.pallas_call(
        lambda *refs: base_kernel(limit, *refs),
        in_specs=[vmem] * (5 + highs),
        out_specs=(pl.BlockSpec(memory_space=pl.ANY), vmem),
        out_shape=(
            jax.ShapeDtypeStruct((layers, rows, width), jnp.float32),
            jax.ShapeDtypeStruct(tile, jnp.float32),
        ),
        scratch_shapes=[
            pltpu.VMEM((layers, rows, width), jnp.float32),
            pltpu.SemaphoreType.DMA((chunks,)),
        ],
        compiler_params=params,
        name="base",
    )(sums, sent, outer_base, averaged, momentum, *all_momenta)
    return (new_base, momentum_next.reshape(outer_momentum.shape))


def solution(mesh):
    replicas, fsdp = mesh.devices.shape
    side = math.isqrt(replicas)
    owners, shards = ("y", "z_hi", "z_lo"), ("x", "core")
    torus = Mesh(
        mesh.devices.reshape(side, side // 2, 2, fsdp // 2, 2), owners + shards
    )
    return jax.shard_map(
        per_device,
        mesh=torus,
        in_specs=(
            P(owners, None, shards, None),
            P(None, shards, None),
            P(None, shards, owners),
        ),
        out_specs=(P(None, shards, None), P(None, shards, owners)),
        check_vma=False,
    )
```

```python
import math

import jax
import jax.numpy as jnp
from jax import lax
from jax.experimental import pallas as pl
from jax.experimental.pallas import tpu as pltpu
from jax.sharding import Mesh, PartitionSpec as P

BLOCK = 128


CODE_RANGE = 448.0
EPSILON = 1e-06
OUTER_RATE = 0.7
NESTEROV = 0.9
CLIP_RMS = 0.001
SUBLANES = 8
VMEM_LIMIT = 8 * 2**20


def split_kernel(params_ref, momentum_ref, blocks_ref):
    ys, lows, entries = blocks_ref.shape[:3]
    highs = entries - 1
    momentum = momentum_ref[...]
    for y in range(ys):
        for low in range(lows):
            for high in range(highs):
                blocks_ref[y, low, high] = params_ref[:, (y * highs + high) * lows + low]
            blocks_ref[y, low, highs] = momentum


def partial_kernel(received_ref, base_ref, packed_ref):
    sources = received_ref.shape[0]
    peers, blocks, groups = packed_ref.shape[:3]
    lows = lax.axis_size("z_lo")
    first = lax.axis_index("y") * (blocks * lows) + lax.axis_index("z_lo")
    for block in range(blocks):
        start = pl.multiple_of((first + block * lows) * BLOCK, BLOCK)
        base = base_ref[:, :, pl.ds(start, BLOCK)].reshape(groups, SUBLANES, BLOCK)
        summed = jnp.zeros(base.shape, jnp.float32)
        for source in range(sources):
            difference = base - received_ref[source, block].astype(jnp.float32)
            largest = jnp.max(jnp.abs(difference), axis=-1, keepdims=True)
            scales = ((largest + EPSILON) / CODE_RANGE).astype(jnp.bfloat16).astype(jnp.float32)
            code_words = (difference / scales).astype(jnp.bfloat16)
            summed = summed + code_words.astype(jnp.float32) * scales
        sent = summed.astype(jnp.bfloat16)
        for peer in range(peers):
            packed_ref[peer, block] = sent


def average_kernel(replicas, packed_ref, received_ref, averaged_ref, rounded_ref, squares_ref, momenta_ref):
    sources, blocks, groups = packed_ref.shape[:3]

    def average(block):
        summed = packed_ref[0, block].astype(jnp.float32)
        for source in range(1, sources):
            summed = summed + packed_ref[source, block].astype(jnp.float32)
        return summed / replicas

    averaged_ref[...] = average(lax.axis_index("z_hi"))
    squares = jnp.zeros((groups, SUBLANES, BLOCK), jnp.float32)
    for block in range(blocks):
        averaged = average(block)
        squares = squares + averaged * averaged
        rounded_ref[block * groups : (block + 1) * groups] = averaged.astype(jnp.bfloat16)
    half = groups // 2
    first = jnp.sum(jnp.sum(jnp.sum(squares[:half], axis=0), axis=0, keepdims=True), axis=-1, keepdims=True)
    second = jnp.sum(jnp.sum(jnp.sum(squares[half:], axis=0), axis=0, keepdims=True), axis=-1, keepdims=True)
    lanes = lax.broadcasted_iota(jnp.int32, squares_ref.shape, 1)
    squares_ref[...] = jnp.where(lanes < BLOCK // 2, first, second)
    momenta_ref[...] = received_ref[:, blocks]


def pack_kernel(sums_ref, rounded_ref, received_ref, sent_ref, momenta_ref):
    peers, entries = sent_ref.shape[:2]
    tile = (SUBLANES, BLOCK)
    rows = lax.broadcasted_iota(jnp.int32, tile, 0)
    rest = jnp.broadcast_to(jnp.sum(sums_ref[...], axis=0, keepdims=True), tile)
    pieces = jnp.zeros(tile, jnp.float32)
    for piece in range(3):
        rounded = rest.astype(jnp.bfloat16).astype(jnp.float32)
        pieces = jnp.where(rows == piece, rounded, pieces)
        rest = rest - rounded
    pieces = pieces.astype(jnp.bfloat16)
    for peer in range(peers):
        sent_ref[peer, : entries - 1] = rounded_ref[...]
        sent_ref[peer, entries - 1] = pieces
    momenta_ref[...] = received_ref[:, received_ref.shape[1] - 1]


def base_kernel(limit, sent_ref, base_ref, averaged_ref, momentum_ref, *refs):
    *momenta_refs, new_base_ref, momentum_next_ref, made_ref, made_momentum_ref, semaphores = refs
    highs = len(momenta_refs)
    groups = averaged_ref.shape[0]
    layers, _, width = base_ref.shape
    lows = lax.axis_size("z_lo")
    ys = sent_ref.shape[0] // lows
    sources, entries = sent_ref.shape[:2]
    sums = sent_ref[0, entries - 1].astype(jnp.float32)
    for source in range(1, sources):
        sums = sums + sent_ref[source, entries - 1].astype(jnp.float32)
    sums = jnp.sum(sums, axis=0, keepdims=True)
    factors = []
    for layer in range(layers):
        share = BLOCK // layers
        total = jnp.max(sums[:, layer * share : (layer + 1) * share], axis=-1, keepdims=True)
        factors.append(jnp.minimum(1.0, limit / (jnp.sqrt(total) + EPSILON)))
    rates = [OUTER_RATE * (1.0 + NESTEROV) * factor for factor in factors]
    momentum_rate = OUTER_RATE * NESTEROV * NESTEROV
    for group in range(groups):
        factor = factors[group * layers // groups]
        made_momentum_ref[group] = NESTEROV * momentum_ref[group] + averaged_ref[group] * factor
    chunks = semaphores.shape[0] - 1
    writes = [pltpu.make_async_copy(made_momentum_ref, momentum_next_ref, semaphores.at[chunks])]
    writes[0].start()
    chunk = width // chunks
    mine = lax.axis_index("z_hi")
    for part in range(chunks):
        for y in range(part * ys // chunks, (part + 1) * ys // chunks):
            for shift in range(highs):
                high = lax.rem(mine + shift, highs)
                for low in range(lows):
                    start = pl.multiple_of(((y * highs + high) * lows + low) * BLOCK, BLOCK)
                    columns = pl.ds(start, BLOCK)
                    source = y * lows + low
                    for group in range(groups):
                        layer, half = divmod(group, groups // layers)
                        rows = pl.ds(half * SUBLANES, SUBLANES)
                        averaged = sent_ref[source, high * groups + group].astype(jnp.float32)
                        momentum = momenta_refs[shift][source, group].astype(jnp.float32)
                        step = (averaged * rates[layer] + momentum * momentum_rate).astype(jnp.bfloat16)
                        made_ref[layer, rows, columns] = (
                            base_ref[layer, rows, columns] - step.astype(jnp.float32)
                        )
        columns = pl.ds(part * chunk, chunk)
        write = pltpu.make_async_copy(
            made_ref.at[:, :, columns], new_base_ref.at[:, :, columns], semaphores.at[part]
        )
        write.start()
        writes.append(write)
    for write in writes:
        write.wait()


def per_device(replica_params, outer_base, outer_momentum):
    ys, highs, lows = lax.axis_size("y"), lax.axis_size("z_hi"), lax.axis_size("z_lo")
    xs, cores = lax.axis_size("x"), lax.axis_size("core")
    replicas = ys * highs * lows
    layers, rows, width = outer_base.shape
    groups = layers * rows // SUBLANES
    limit = CLIP_RMS * math.sqrt(rows * xs * cores * width)
    params = pltpu.CompilerParams(vmem_limit_bytes=VMEM_LIMIT)
    tile = (groups, SUBLANES, BLOCK)
    owners = ys * lows
    anywhere = pl.BlockSpec(memory_space=pl.ANY)
    momentum = outer_momentum.reshape(tile)

    grouped = replica_params.reshape(groups, SUBLANES, replicas, BLOCK).transpose(0, 2, 1, 3)
    blocks = pl.pallas_call(
        split_kernel,
        out_shape=jax.ShapeDtypeStruct((ys, lows, highs + 1, *tile), replica_params.dtype),
        compiler_params=params,
        name="split",
    )(grouped, momentum.astype(jnp.bfloat16))
    received = lax.all_to_all(
        blocks.reshape(owners, highs + 1, *tile), ("y", "z_lo"), 0, 0, tiled=True
    )
    packed = pl.pallas_call(
        partial_kernel,
        out_shape=jax.ShapeDtypeStruct((highs, highs, *tile), jnp.bfloat16),
        compiler_params=params,
        name="partial",
    )(received, outer_base)
    packed = lax.all_to_all(packed, "z_hi", 0, 0, tiled=True)

    shards = xs * cores
    spread = jax.ShapeDtypeStruct((owners, *tile), jnp.bfloat16)
    averaged, rounded, squares, early_momenta = pl.pallas_call(
        lambda *refs: average_kernel(replicas, *refs),
        out_shape=(
            jax.ShapeDtypeStruct(tile, jnp.float32),
            jax.ShapeDtypeStruct((highs * groups, SUBLANES, BLOCK), jnp.bfloat16),
            jax.ShapeDtypeStruct((shards, BLOCK), jnp.float32),
            spread,
        ),
        compiler_params=params,
        name="average",
    )(packed, received)
    sums = lax.all_to_all(
        squares.reshape(shards, 1, BLOCK), ("x", "core"), 0, 0, tiled=True
    ).reshape(shards, BLOCK)
    sent, momenta = pl.pallas_call(
        pack_kernel,
        out_shape=(
            jax.ShapeDtypeStruct((owners, highs * groups + 1, SUBLANES, BLOCK), jnp.bfloat16),
            spread,
        ),
        compiler_params=params,
        name="pack",
    )(sums, rounded, received)
    sent = lax.all_to_all(sent, ("y", "z_lo"), 0, 0, tiled=True)
    all_momenta = [momenta] + [
        lax.ppermute(
            early_momenta if shift == highs // 2 else momenta,
            "z_hi",
            [(i, (i - shift) % highs) for i in range(highs)],
        )
        for shift in range(1, highs)
    ]

    chunks = 8
    vmem = pl.BlockSpec(memory_space=pltpu.VMEM)
    new_base, momentum_next = pl.pallas_call(
        lambda *refs: base_kernel(limit, *refs),
        in_specs=[vmem] * (4 + highs),
        out_specs=(anywhere, anywhere),
        out_shape=(
            jax.ShapeDtypeStruct((layers, rows, width), jnp.float32),
            jax.ShapeDtypeStruct(tile, jnp.float32),
        ),
        scratch_shapes=[
            pltpu.VMEM((layers, rows, width), jnp.float32),
            pltpu.VMEM(tile, jnp.float32),
            pltpu.SemaphoreType.DMA((chunks + 1,)),
        ],
        compiler_params=params,
        name="base",
    )(sent, outer_base, averaged, momentum, *all_momenta)
    return (new_base, momentum_next.reshape(outer_momentum.shape))


def solution(mesh):
    replicas, fsdp = mesh.devices.shape
    side = math.isqrt(replicas)
    owners, shards = ("y", "z_hi", "z_lo"), ("x", "core")
    torus = Mesh(
        mesh.devices.reshape(side, side // 2, 2, fsdp // 2, 2), owners + shards
    )
    return jax.shard_map(
        per_device,
        mesh=torus,
        in_specs=(
            P(owners, None, shards, None),
            P(None, shards, None),
            P(None, shards, owners),
        ),
        out_specs=(P(None, shards, None), P(None, shards, owners)),
        check_vma=False,
    )
```

```python
import math

import jax
import jax.numpy as jnp
from jax import lax
from jax.experimental import pallas as pl
from jax.experimental.pallas import tpu as pltpu
from jax.sharding import Mesh, PartitionSpec as P

BLOCK = 128


CODE_RANGE = 448.0
EPSILON = 1e-06
OUTER_RATE = 0.7
NESTEROV = 0.9
CLIP_RMS = 0.001
SUBLANES = 8
VMEM_LIMIT = 8 * 2**20


def split_kernel(params_ref, momentum_ref, blocks_ref):
    ys, lows, entries = blocks_ref.shape[:3]
    highs = entries - 1
    momentum = momentum_ref[...]
    for y in range(ys):
        for low in range(lows):
            for high in range(highs):
                blocks_ref[y, low, high] = params_ref[:, (y * highs + high) * lows + low]
            blocks_ref[y, low, highs] = momentum


def partial_kernel(received_ref, base_ref, packed_ref):
    sources = received_ref.shape[0]
    peers, blocks, groups = packed_ref.shape[:3]
    lows = lax.axis_size("z_lo")
    first = lax.axis_index("y") * (blocks * lows) + lax.axis_index("z_lo")
    for block in range(blocks):
        start = pl.multiple_of((first + block * lows) * BLOCK, BLOCK)
        base = base_ref[:, :, pl.ds(start, BLOCK)].reshape(groups, SUBLANES, BLOCK)
        summed = jnp.zeros(base.shape, jnp.float32)
        for source in range(sources):
            difference = base - received_ref[source, block].astype(jnp.float32)
            largest = jnp.max(jnp.abs(difference), axis=-1, keepdims=True)
            scales = ((largest + EPSILON) / CODE_RANGE).astype(jnp.bfloat16).astype(jnp.float32)
            code_words = (difference / scales).astype(jnp.bfloat16)
            summed = summed + code_words.astype(jnp.float32) * scales
        sent = summed.astype(jnp.bfloat16)
        for peer in range(peers):
            packed_ref[peer, block] = sent


def average_kernel(replicas, packed_ref, received_ref, averaged_ref, sent_ref, momenta_ref):
    sources, blocks, groups = packed_ref.shape[:3]
    peers = sent_ref.shape[0]

    def average(block):
        summed = packed_ref[0, block].astype(jnp.float32)
        for source in range(1, sources):
            summed = summed + packed_ref[source, block].astype(jnp.float32)
        return summed / replicas

    averaged_ref[...] = average(lax.axis_index("z_hi"))
    squares = jnp.zeros((groups, SUBLANES, BLOCK), jnp.float32)
    for block in range(blocks):
        averaged = average(block)
        squares = squares + averaged * averaged
        sent = averaged.astype(jnp.bfloat16)
        for peer in range(peers):
            sent_ref[peer, block * groups : (block + 1) * groups] = sent
    half = groups // 2
    first = jnp.sum(jnp.sum(jnp.sum(squares[:half], axis=0), axis=0, keepdims=True), axis=-1, keepdims=True)
    second = jnp.sum(jnp.sum(jnp.sum(squares[half:], axis=0), axis=0, keepdims=True), axis=-1, keepdims=True)
    tile = (SUBLANES, BLOCK)
    lanes = lax.broadcasted_iota(jnp.int32, tile, 1)
    rows = lax.broadcasted_iota(jnp.int32, tile, 0)
    rest = jnp.where(lanes < BLOCK // 2, first, second)
    pieces = jnp.zeros(tile, jnp.float32)
    for piece in range(3):
        rounded = rest.astype(jnp.bfloat16).astype(jnp.float32)
        pieces = jnp.where(rows == piece, rounded, pieces)
        rest = rest - rounded
    pieces = pieces.astype(jnp.bfloat16)
    for peer in range(peers):
        sent_ref[peer, blocks * groups] = pieces
        momenta_ref[peer] = received_ref[peer, blocks]


def sum_kernel(sent_ref, sums_ref):
    sources, tiles = sent_ref.shape[:2]
    total = sent_ref[0, tiles - 1].astype(jnp.float32)
    for source in range(1, sources):
        total = total + sent_ref[source, tiles - 1].astype(jnp.float32)
    sums_ref[...] = jnp.broadcast_to(jnp.sum(total, axis=0, keepdims=True), sums_ref.shape)


def base_kernel(limit, sums_ref, sent_ref, base_ref, averaged_ref, momentum_ref, *refs):
    *momenta_refs, new_base_ref, momentum_next_ref, made_ref, made_momentum_ref, semaphores = refs
    highs = len(momenta_refs)
    groups = averaged_ref.shape[0]
    layers, _, width = base_ref.shape
    lows = lax.axis_size("z_lo")
    ys = sent_ref.shape[0] // lows
    sums = jnp.sum(sums_ref[...], axis=0, keepdims=True)
    factors = []
    for layer in range(layers):
        share = BLOCK // layers
        total = jnp.max(sums[:, layer * share : (layer + 1) * share], axis=-1, keepdims=True)
        factors.append(jnp.minimum(1.0, limit / (jnp.sqrt(total) + EPSILON)))
    rates = [OUTER_RATE * (1.0 + NESTEROV) * factor for factor in factors]
    momentum_rate = OUTER_RATE * NESTEROV * NESTEROV
    for group in range(groups):
        factor = factors[group * layers // groups]
        made_momentum_ref[group] = NESTEROV * momentum_ref[group] + averaged_ref[group] * factor
    chunks = semaphores.shape[0] - 1
    writes = [pltpu.make_async_copy(made_momentum_ref, momentum_next_ref, semaphores.at[chunks])]
    writes[0].start()
    chunk = width // chunks
    mine = lax.axis_index("z_hi")
    for part in range(chunks):
        for y in range(part * ys // chunks, (part + 1) * ys // chunks):
            for shift in range(highs):
                high = lax.rem(mine + shift, highs)
                for low in range(lows):
                    start = pl.multiple_of(((y * highs + high) * lows + low) * BLOCK, BLOCK)
                    columns = pl.ds(start, BLOCK)
                    source = y * lows + low
                    for group in range(groups):
                        layer, half = divmod(group, groups // layers)
                        rows = pl.ds(half * SUBLANES, SUBLANES)
                        averaged = sent_ref[source, high * groups + group].astype(jnp.float32)
                        momentum = momenta_refs[shift][source, group].astype(jnp.float32)
                        step = (averaged * rates[layer] + momentum * momentum_rate).astype(jnp.bfloat16)
                        made_ref[layer, rows, columns] = (
                            base_ref[layer, rows, columns] - step.astype(jnp.float32)
                        )
        columns = pl.ds(part * chunk, chunk)
        write = pltpu.make_async_copy(
            made_ref.at[:, :, columns], new_base_ref.at[:, :, columns], semaphores.at[part]
        )
        write.start()
        writes.append(write)
    for write in writes:
        write.wait()


def per_device(replica_params, outer_base, outer_momentum):
    ys, highs, lows = lax.axis_size("y"), lax.axis_size("z_hi"), lax.axis_size("z_lo")
    xs, cores = lax.axis_size("x"), lax.axis_size("core")
    replicas = ys * highs * lows
    layers, rows, width = outer_base.shape
    groups = layers * rows // SUBLANES
    limit = CLIP_RMS * math.sqrt(rows * xs * cores * width)
    params = pltpu.CompilerParams(vmem_limit_bytes=VMEM_LIMIT)
    tile = (groups, SUBLANES, BLOCK)
    owners = ys * lows
    anywhere = pl.BlockSpec(memory_space=pl.ANY)
    momentum = outer_momentum.reshape(tile)

    grouped = replica_params.reshape(groups, SUBLANES, replicas, BLOCK).transpose(0, 2, 1, 3)
    blocks = pl.pallas_call(
        split_kernel,
        out_shape=jax.ShapeDtypeStruct((ys, lows, highs + 1, *tile), replica_params.dtype),
        compiler_params=params,
        name="split",
    )(grouped, momentum.astype(jnp.bfloat16))
    received = lax.all_to_all(
        blocks.reshape(owners, highs + 1, *tile), ("y", "z_lo"), 0, 0, tiled=True
    )
    packed = pl.pallas_call(
        partial_kernel,
        out_shape=jax.ShapeDtypeStruct((highs, highs, *tile), jnp.bfloat16),
        compiler_params=params,
        name="partial",
    )(received, outer_base)
    packed = lax.all_to_all(packed, "z_hi", 0, 0, tiled=True)

    averaged, sent, momenta = pl.pallas_call(
        lambda *refs: average_kernel(replicas, *refs),
        out_shape=(
            jax.ShapeDtypeStruct(tile, jnp.float32),
            jax.ShapeDtypeStruct((owners, highs * groups + 1, SUBLANES, BLOCK), jnp.bfloat16),
            jax.ShapeDtypeStruct((owners, *tile), jnp.bfloat16),
        ),
        compiler_params=params,
        name="average",
    )(packed, received)
    sent = lax.all_to_all(sent, ("y", "z_lo"), 0, 0, tiled=True)
    all_momenta = [momenta] + [
        lax.ppermute(momenta, "z_hi", [(i, (i - shift) % highs) for i in range(highs)])
        for shift in range(1, highs)
    ]
    shards = xs * cores
    sums = pl.pallas_call(
        sum_kernel,
        out_shape=jax.ShapeDtypeStruct((shards, BLOCK), jnp.float32),
        compiler_params=params,
        name="sum",
    )(sent)
    sums = lax.all_to_all(
        sums.reshape(shards, 1, BLOCK), ("x", "core"), 0, 0, tiled=True
    ).reshape(shards, BLOCK)

    chunks = 8
    vmem = pl.BlockSpec(memory_space=pltpu.VMEM)
    new_base, momentum_next = pl.pallas_call(
        lambda *refs: base_kernel(limit, *refs),
        in_specs=[vmem] * (5 + highs),
        out_specs=(anywhere, anywhere),
        out_shape=(
            jax.ShapeDtypeStruct((layers, rows, width), jnp.float32),
            jax.ShapeDtypeStruct(tile, jnp.float32),
        ),
        scratch_shapes=[
            pltpu.VMEM((layers, rows, width), jnp.float32),
            pltpu.VMEM(tile, jnp.float32),
            pltpu.SemaphoreType.DMA((chunks + 1,)),
        ],
        compiler_params=params,
        name="base",
    )(sums, sent, outer_base, averaged, momentum, *all_momenta)
    return (new_base, momentum_next.reshape(outer_momentum.shape))


def solution(mesh):
    replicas, fsdp = mesh.devices.shape
    side = math.isqrt(replicas)
    owners, shards = ("y", "z_hi", "z_lo"), ("x", "core")
    torus = Mesh(
        mesh.devices.reshape(side, side // 2, 2, fsdp // 2, 2), owners + shards
    )
    return jax.shard_map(
        per_device,
        mesh=torus,
        in_specs=(
            P(owners, None, shards, None),
            P(None, shards, None),
            P(None, shards, owners),
        ),
        out_specs=(P(None, shards, None), P(None, shards, owners)),
        check_vma=False,
    )
```

```python
import math

import jax
import jax.numpy as jnp
from jax import lax
from jax.experimental import pallas as pl
from jax.experimental.pallas import tpu as pltpu
from jax.sharding import Mesh, PartitionSpec as P

BLOCK = 128


CODE_RANGE = 448.0
EPSILON = 1e-06
OUTER_RATE = 0.7
NESTEROV = 0.9
CLIP_RMS = 0.001
SUBLANES = 8
VMEM_LIMIT = 8 * 2**20


def split_kernel(params_ref, momentum_ref, blocks_ref):
    ys, lows, entries = blocks_ref.shape[:3]
    highs = entries - 1
    momentum = momentum_ref[...]
    for y in range(ys):
        for low in range(lows):
            for high in range(highs):
                blocks_ref[y, low, high] = params_ref[:, (y * highs + high) * lows + low]
            blocks_ref[y, low, highs] = momentum


def partial_kernel(received_ref, base_ref, packed_ref):
    sources = received_ref.shape[0]
    peers, blocks, groups = packed_ref.shape[:3]
    lows = lax.axis_size("z_lo")
    first = lax.axis_index("y") * (blocks * lows) + lax.axis_index("z_lo")
    for block in range(blocks):
        start = pl.multiple_of((first + block * lows) * BLOCK, BLOCK)
        base = base_ref[:, :, pl.ds(start, BLOCK)].reshape(groups, SUBLANES, BLOCK)
        summed = jnp.zeros(base.shape, jnp.float32)
        for source in range(sources):
            difference = base - received_ref[source, block].astype(jnp.float32)
            largest = jnp.max(jnp.abs(difference), axis=-1, keepdims=True)
            scales = ((largest + EPSILON) / CODE_RANGE).astype(jnp.bfloat16).astype(jnp.float32)
            code_words = (difference / scales).astype(jnp.bfloat16)
            summed = summed + code_words.astype(jnp.float32) * scales
        sent = summed.astype(jnp.bfloat16)
        for peer in range(peers):
            packed_ref[peer, block] = sent


def average_kernel(replicas, packed_ref, received_ref, averaged_ref, sent_ref, momenta_ref, made_ref, semaphores):
    sources, blocks, groups = packed_ref.shape[:3]
    peers = sent_ref.shape[0]

    def average(block):
        summed = packed_ref[0, block].astype(jnp.float32)
        for source in range(1, sources):
            summed = summed + packed_ref[source, block].astype(jnp.float32)
        return summed / replicas

    squares = jnp.zeros((groups, SUBLANES, BLOCK), jnp.float32)
    for block in range(blocks):
        averaged = average(block)
        squares = squares + averaged * averaged
        made_ref[block * groups : (block + 1) * groups] = averaged.astype(jnp.bfloat16)
    half = groups // 2
    first = jnp.sum(jnp.sum(jnp.sum(squares[:half], axis=0), axis=0, keepdims=True), axis=-1, keepdims=True)
    second = jnp.sum(jnp.sum(jnp.sum(squares[half:], axis=0), axis=0, keepdims=True), axis=-1, keepdims=True)
    tile = (SUBLANES, BLOCK)
    lanes = lax.broadcasted_iota(jnp.int32, tile, 1)
    rows = lax.broadcasted_iota(jnp.int32, tile, 0)
    rest = jnp.where(lanes < BLOCK // 2, first, second)
    pieces = jnp.zeros(tile, jnp.float32)
    for piece in range(3):
        rounded = rest.astype(jnp.bfloat16).astype(jnp.float32)
        pieces = jnp.where(rows == piece, rounded, pieces)
        rest = rest - rounded
    made_ref[blocks * groups] = pieces.astype(jnp.bfloat16)
    writes = [
        pltpu.make_async_copy(made_ref, sent_ref.at[peer], semaphores.at[peer])
        for peer in range(peers)
    ]
    for write in writes:
        write.start()
    momenta_ref[...] = received_ref[:, blocks]
    averaged_ref[...] = average(lax.axis_index("z_hi"))
    for write in writes:
        write.wait()


def sum_kernel(sent_ref, sums_ref):
    sources, tiles = sent_ref.shape[:2]
    total = sent_ref[0, tiles - 1].astype(jnp.float32)
    for source in range(1, sources):
        total = total + sent_ref[source, tiles - 1].astype(jnp.float32)
    sums_ref[...] = jnp.broadcast_to(jnp.sum(total, axis=0, keepdims=True), sums_ref.shape)


def base_kernel(limit, sums_ref, sent_ref, base_ref, averaged_ref, momentum_ref, *refs):
    *momenta_refs, new_base_ref, momentum_next_ref, made_ref, made_momentum_ref, semaphores = refs
    highs = len(momenta_refs)
    groups = averaged_ref.shape[0]
    layers, _, width = base_ref.shape
    lows = lax.axis_size("z_lo")
    ys = sent_ref.shape[0] // lows
    sums = jnp.sum(sums_ref[...], axis=0, keepdims=True)
    factors = []
    for layer in range(layers):
        share = BLOCK // layers
        total = jnp.max(sums[:, layer * share : (layer + 1) * share], axis=-1, keepdims=True)
        factors.append(jnp.minimum(1.0, limit / (jnp.sqrt(total) + EPSILON)))
    rates = [OUTER_RATE * (1.0 + NESTEROV) * factor for factor in factors]
    momentum_rate = OUTER_RATE * NESTEROV * NESTEROV
    for group in range(groups):
        factor = factors[group * layers // groups]
        made_momentum_ref[group] = NESTEROV * momentum_ref[group] + averaged_ref[group] * factor
    chunks = semaphores.shape[0] - 1
    writes = [pltpu.make_async_copy(made_momentum_ref, momentum_next_ref, semaphores.at[chunks])]
    writes[0].start()
    chunk = width // chunks
    mine = lax.axis_index("z_hi")
    for part in range(chunks):
        for y in range(part * ys // chunks, (part + 1) * ys // chunks):
            for shift in range(highs):
                high = lax.rem(mine + shift, highs)
                for low in range(lows):
                    start = pl.multiple_of(((y * highs + high) * lows + low) * BLOCK, BLOCK)
                    columns = pl.ds(start, BLOCK)
                    source = y * lows + low
                    for group in range(groups):
                        layer, half = divmod(group, groups // layers)
                        rows = pl.ds(half * SUBLANES, SUBLANES)
                        averaged = sent_ref[source, high * groups + group].astype(jnp.float32)
                        momentum = momenta_refs[shift][source, group].astype(jnp.float32)
                        step = (averaged * rates[layer] + momentum * momentum_rate).astype(jnp.bfloat16)
                        made_ref[layer, rows, columns] = (
                            base_ref[layer, rows, columns] - step.astype(jnp.float32)
                        )
        columns = pl.ds(part * chunk, chunk)
        write = pltpu.make_async_copy(
            made_ref.at[:, :, columns], new_base_ref.at[:, :, columns], semaphores.at[part]
        )
        write.start()
        writes.append(write)
    for write in writes:
        write.wait()


def per_device(replica_params, outer_base, outer_momentum):
    ys, highs, lows = lax.axis_size("y"), lax.axis_size("z_hi"), lax.axis_size("z_lo")
    xs, cores = lax.axis_size("x"), lax.axis_size("core")
    replicas = ys * highs * lows
    layers, rows, width = outer_base.shape
    groups = layers * rows // SUBLANES
    limit = CLIP_RMS * math.sqrt(rows * xs * cores * width)
    params = pltpu.CompilerParams(vmem_limit_bytes=VMEM_LIMIT)
    tile = (groups, SUBLANES, BLOCK)
    owners = ys * lows
    anywhere = pl.BlockSpec(memory_space=pl.ANY)
    vmem = pl.BlockSpec(memory_space=pltpu.VMEM)
    momentum = outer_momentum.reshape(tile)

    grouped = replica_params.reshape(groups, SUBLANES, replicas, BLOCK).transpose(0, 2, 1, 3)
    blocks = pl.pallas_call(
        split_kernel,
        out_shape=jax.ShapeDtypeStruct((ys, lows, highs + 1, *tile), replica_params.dtype),
        compiler_params=params,
        name="split",
    )(grouped, momentum.astype(jnp.bfloat16))
    received = lax.all_to_all(
        blocks.reshape(owners, highs + 1, *tile), ("y", "z_lo"), 0, 0, tiled=True
    )
    packed = pl.pallas_call(
        partial_kernel,
        out_shape=jax.ShapeDtypeStruct((highs, highs, *tile), jnp.bfloat16),
        compiler_params=params,
        name="partial",
    )(received, outer_base)
    packed = lax.all_to_all(packed, "z_hi", 0, 0, tiled=True)

    averaged, sent, momenta = pl.pallas_call(
        lambda *refs: average_kernel(replicas, *refs),
        out_shape=(
            jax.ShapeDtypeStruct(tile, jnp.float32),
            jax.ShapeDtypeStruct((owners, highs * groups + 1, SUBLANES, BLOCK), jnp.bfloat16),
            jax.ShapeDtypeStruct((owners, *tile), jnp.bfloat16),
        ),
        out_specs=(vmem, anywhere, vmem),
        scratch_shapes=[
            pltpu.VMEM((highs * groups + 1, SUBLANES, BLOCK), jnp.bfloat16),
            pltpu.SemaphoreType.DMA((owners,)),
        ],
        compiler_params=params,
        name="average",
    )(packed, received)
    sent = lax.all_to_all(sent, ("y", "z_lo"), 0, 0, tiled=True)
    all_momenta = [momenta] + [
        lax.ppermute(momenta, "z_hi", [(i, (i - shift) % highs) for i in range(highs)])
        for shift in range(1, highs)
    ]
    shards = xs * cores
    sums = pl.pallas_call(
        sum_kernel,
        out_shape=jax.ShapeDtypeStruct((shards, BLOCK), jnp.float32),
        compiler_params=params,
        name="sum",
    )(sent)
    sums = lax.all_to_all(
        sums.reshape(shards, 1, BLOCK), ("x", "core"), 0, 0, tiled=True
    ).reshape(shards, BLOCK)

    chunks = 8
    new_base, momentum_next = pl.pallas_call(
        lambda *refs: base_kernel(limit, *refs),
        in_specs=[vmem] * (5 + highs),
        out_specs=(anywhere, anywhere),
        out_shape=(
            jax.ShapeDtypeStruct((layers, rows, width), jnp.float32),
            jax.ShapeDtypeStruct(tile, jnp.float32),
        ),
        scratch_shapes=[
            pltpu.VMEM((layers, rows, width), jnp.float32),
            pltpu.VMEM(tile, jnp.float32),
            pltpu.SemaphoreType.DMA((chunks + 1,)),
        ],
        compiler_params=params,
        name="base",
    )(sums, sent, outer_base, averaged, momentum, *all_momenta)
    return (new_base, momentum_next.reshape(outer_momentum.shape))


def solution(mesh):
    replicas, fsdp = mesh.devices.shape
    side = math.isqrt(replicas)
    owners, shards = ("y", "z_hi", "z_lo"), ("x", "core")
    torus = Mesh(
        mesh.devices.reshape(side, side // 2, 2, fsdp // 2, 2), owners + shards
    )
    return jax.shard_map(
        per_device,
        mesh=torus,
        in_specs=(
            P(owners, None, shards, None),
            P(None, shards, None),
            P(None, shards, owners),
        ),
        out_specs=(P(None, shards, None), P(None, shards, owners)),
        check_vma=False,
    )
```

```python
import math

import jax
import jax.numpy as jnp
from jax import lax
from jax.experimental import pallas as pl
from jax.experimental.pallas import tpu as pltpu
from jax.sharding import Mesh, PartitionSpec as P

BLOCK = 128


CODE_RANGE = 448.0
EPSILON = 1e-06
OUTER_RATE = 0.7
NESTEROV = 0.9
CLIP_RMS = 0.001
SUBLANES = 8
VMEM_LIMIT = 8 * 2**20


def split_kernel(first_ref, second_ref, momentum_ref, blocks_ref):
    ys, lows, entries = blocks_ref.shape[:3]
    highs = entries - 1
    momentum = momentum_ref[...]
    for y in range(ys):
        for low in range(lows):
            for high in range(highs):
                owner = (y * highs + high) * lows + low
                half = first_ref.shape[0]
                blocks_ref[y, low, high, :half] = first_ref[:, owner]
                blocks_ref[y, low, high, half:] = second_ref[:, owner]
            blocks_ref[y, low, highs] = momentum


def partial_kernel(received_ref, base_ref, packed_ref):
    sources = received_ref.shape[0]
    peers, blocks, groups = packed_ref.shape[:3]
    lows = lax.axis_size("z_lo")
    first = lax.axis_index("y") * (blocks * lows) + lax.axis_index("z_lo")
    for block in range(blocks):
        start = pl.multiple_of((first + block * lows) * BLOCK, BLOCK)
        base = base_ref[:, :, pl.ds(start, BLOCK)].reshape(groups, SUBLANES, BLOCK)
        summed = jnp.zeros(base.shape, jnp.float32)
        for source in range(sources):
            difference = base - received_ref[source, block].astype(jnp.float32)
            largest = jnp.max(jnp.abs(difference), axis=-1, keepdims=True)
            scales = ((largest + EPSILON) / CODE_RANGE).astype(jnp.bfloat16).astype(jnp.float32)
            code_words = (difference / scales).astype(jnp.bfloat16)
            summed = summed + code_words.astype(jnp.float32) * scales
        sent = summed.astype(jnp.bfloat16)
        for peer in range(peers):
            packed_ref[peer, block] = sent


def average_kernel(replicas, packed_ref, received_ref, averaged_ref, sent_ref, momenta_ref, made_ref, semaphores):
    sources, blocks, groups = packed_ref.shape[:3]
    peers = sent_ref.shape[0]

    def average(block):
        summed = packed_ref[0, block].astype(jnp.float32)
        for source in range(1, sources):
            summed = summed + packed_ref[source, block].astype(jnp.float32)
        return summed / replicas

    squares = jnp.zeros((groups, SUBLANES, BLOCK), jnp.float32)
    for block in range(blocks):
        averaged = average(block)
        squares = squares + averaged * averaged
        made_ref[block * groups : (block + 1) * groups] = averaged.astype(jnp.bfloat16)
    half = groups // 2
    first = jnp.sum(jnp.sum(jnp.sum(squares[:half], axis=0), axis=0, keepdims=True), axis=-1, keepdims=True)
    second = jnp.sum(jnp.sum(jnp.sum(squares[half:], axis=0), axis=0, keepdims=True), axis=-1, keepdims=True)
    tile = (SUBLANES, BLOCK)
    lanes = lax.broadcasted_iota(jnp.int32, tile, 1)
    rows = lax.broadcasted_iota(jnp.int32, tile, 0)
    rest = jnp.where(lanes < BLOCK // 2, first, second)
    pieces = jnp.zeros(tile, jnp.float32)
    for piece in range(3):
        rounded = rest.astype(jnp.bfloat16).astype(jnp.float32)
        pieces = jnp.where(rows == piece, rounded, pieces)
        rest = rest - rounded
    made_ref[blocks * groups] = pieces.astype(jnp.bfloat16)
    writes = [
        pltpu.make_async_copy(made_ref, sent_ref.at[peer], semaphores.at[peer])
        for peer in range(peers)
    ]
    for write in writes:
        write.start()
    momenta_ref[...] = received_ref[:, blocks]
    averaged_ref[...] = average(lax.axis_index("z_hi"))
    for write in writes:
        write.wait()


def sum_kernel(sent_ref, sums_ref):
    sources, tiles = sent_ref.shape[:2]
    total = sent_ref[0, tiles - 1].astype(jnp.float32)
    for source in range(1, sources):
        total = total + sent_ref[source, tiles - 1].astype(jnp.float32)
    sums_ref[...] = jnp.broadcast_to(jnp.sum(total, axis=0, keepdims=True), sums_ref.shape)


def base_kernel(limit, sums_ref, sent_ref, base_ref, averaged_ref, momentum_ref, *refs):
    *momenta_refs, new_base_ref, momentum_next_ref, made_ref, made_momentum_ref, semaphores = refs
    highs = len(momenta_refs)
    groups = averaged_ref.shape[0]
    layers, _, width = base_ref.shape
    lows = lax.axis_size("z_lo")
    ys = sent_ref.shape[0] // lows
    sums = jnp.sum(sums_ref[...], axis=0, keepdims=True)
    factors = []
    for layer in range(layers):
        share = BLOCK // layers
        total = jnp.max(sums[:, layer * share : (layer + 1) * share], axis=-1, keepdims=True)
        factors.append(jnp.minimum(1.0, limit / (jnp.sqrt(total) + EPSILON)))
    rates = [OUTER_RATE * (1.0 + NESTEROV) * factor for factor in factors]
    momentum_rate = OUTER_RATE * NESTEROV * NESTEROV
    for group in range(groups):
        factor = factors[group * layers // groups]
        made_momentum_ref[group] = NESTEROV * momentum_ref[group] + averaged_ref[group] * factor
    chunks = semaphores.shape[0] - 1
    writes = [pltpu.make_async_copy(made_momentum_ref, momentum_next_ref, semaphores.at[chunks])]
    writes[0].start()
    chunk = width // chunks
    mine = lax.axis_index("z_hi")
    for part in range(chunks):
        for y in range(part * ys // chunks, (part + 1) * ys // chunks):
            for shift in range(highs):
                high = lax.rem(mine + shift, highs)
                for low in range(lows):
                    start = pl.multiple_of(((y * highs + high) * lows + low) * BLOCK, BLOCK)
                    columns = pl.ds(start, BLOCK)
                    source = y * lows + low
                    for group in range(groups):
                        layer, half = divmod(group, groups // layers)
                        rows = pl.ds(half * SUBLANES, SUBLANES)
                        averaged = sent_ref[source, high * groups + group].astype(jnp.float32)
                        momentum = momenta_refs[shift][source, group].astype(jnp.float32)
                        step = (averaged * rates[layer] + momentum * momentum_rate).astype(jnp.bfloat16)
                        made_ref[layer, rows, columns] = (
                            base_ref[layer, rows, columns] - step.astype(jnp.float32)
                        )
        columns = pl.ds(part * chunk, chunk)
        write = pltpu.make_async_copy(
            made_ref.at[:, :, columns], new_base_ref.at[:, :, columns], semaphores.at[part]
        )
        write.start()
        writes.append(write)
    for write in writes:
        write.wait()


def per_device(replica_params, outer_base, outer_momentum):
    ys, highs, lows = lax.axis_size("y"), lax.axis_size("z_hi"), lax.axis_size("z_lo")
    xs, cores = lax.axis_size("x"), lax.axis_size("core")
    replicas = ys * highs * lows
    layers, rows, width = outer_base.shape
    groups = layers * rows // SUBLANES
    limit = CLIP_RMS * math.sqrt(rows * xs * cores * width)
    params = pltpu.CompilerParams(vmem_limit_bytes=VMEM_LIMIT)
    tile = (groups, SUBLANES, BLOCK)
    owners = ys * lows
    anywhere = pl.BlockSpec(memory_space=pl.ANY)
    vmem = pl.BlockSpec(memory_space=pltpu.VMEM)
    momentum = outer_momentum.reshape(tile)

    grouped = replica_params.reshape(groups, SUBLANES, replicas, BLOCK).transpose(0, 2, 1, 3)
    blocks = pl.pallas_call(
        split_kernel,
        out_shape=jax.ShapeDtypeStruct((ys, lows, highs + 1, *tile), replica_params.dtype),
        compiler_params=params,
        name="split",
    )(grouped[: groups // 2], grouped[groups // 2 :], momentum.astype(jnp.bfloat16))
    received = lax.all_to_all(
        blocks.reshape(owners, highs + 1, *tile), ("y", "z_lo"), 0, 0, tiled=True
    )
    packed = pl.pallas_call(
        partial_kernel,
        out_shape=jax.ShapeDtypeStruct((highs, highs, *tile), jnp.bfloat16),
        compiler_params=params,
        name="partial",
    )(received, outer_base)
    packed = lax.all_to_all(packed, "z_hi", 0, 0, tiled=True)

    averaged, sent, momenta = pl.pallas_call(
        lambda *refs: average_kernel(replicas, *refs),
        out_shape=(
            jax.ShapeDtypeStruct(tile, jnp.float32),
            jax.ShapeDtypeStruct((owners, highs * groups + 1, SUBLANES, BLOCK), jnp.bfloat16),
            jax.ShapeDtypeStruct((owners, *tile), jnp.bfloat16),
        ),
        out_specs=(vmem, anywhere, vmem),
        scratch_shapes=[
            pltpu.VMEM((highs * groups + 1, SUBLANES, BLOCK), jnp.bfloat16),
            pltpu.SemaphoreType.DMA((owners,)),
        ],
        compiler_params=params,
        name="average",
    )(packed, received)
    sent = lax.all_to_all(sent, ("y", "z_lo"), 0, 0, tiled=True)
    all_momenta = [momenta] + [
        lax.ppermute(momenta, "z_hi", [(i, (i - shift) % highs) for i in range(highs)])
        for shift in range(1, highs)
    ]
    shards = xs * cores
    sums = pl.pallas_call(
        sum_kernel,
        out_shape=jax.ShapeDtypeStruct((shards, BLOCK), jnp.float32),
        compiler_params=params,
        name="sum",
    )(sent)
    sums = lax.all_to_all(
        sums.reshape(shards, 1, BLOCK), ("x", "core"), 0, 0, tiled=True
    ).reshape(shards, BLOCK)

    chunks = 8
    new_base, momentum_next = pl.pallas_call(
        lambda *refs: base_kernel(limit, *refs),
        in_specs=[vmem] * (5 + highs),
        out_specs=(anywhere, anywhere),
        out_shape=(
            jax.ShapeDtypeStruct((layers, rows, width), jnp.float32),
            jax.ShapeDtypeStruct(tile, jnp.float32),
        ),
        scratch_shapes=[
            pltpu.VMEM((layers, rows, width), jnp.float32),
            pltpu.VMEM(tile, jnp.float32),
            pltpu.SemaphoreType.DMA((chunks + 1,)),
        ],
        compiler_params=params,
        name="base",
    )(sums, sent, outer_base, averaged, momentum, *all_momenta)
    return (new_base, momentum_next.reshape(outer_momentum.shape))


def solution(mesh):
    replicas, fsdp = mesh.devices.shape
    side = math.isqrt(replicas)
    owners, shards = ("y", "z_hi", "z_lo"), ("x", "core")
    torus = Mesh(
        mesh.devices.reshape(side, side // 2, 2, fsdp // 2, 2), owners + shards
    )
    return jax.shard_map(
        per_device,
        mesh=torus,
        in_specs=(
            P(owners, None, shards, None),
            P(None, shards, None),
            P(None, shards, owners),
        ),
        out_specs=(P(None, shards, None), P(None, shards, owners)),
        check_vma=False,
    )
```

```python
import math

import jax
import jax.numpy as jnp
from jax import lax
from jax.experimental import pallas as pl
from jax.experimental.pallas import tpu as pltpu
from jax.sharding import Mesh, PartitionSpec as P

BLOCK = 128


CODE_RANGE = 448.0
EPSILON = 1e-06
OUTER_RATE = 0.7
NESTEROV = 0.9
CLIP_RMS = 0.001
SUBLANES = 8
VMEM_LIMIT = 8 * 2**20


def split_kernel(params_ref, momentum_ref, blocks_ref):
    ys, lows, entries = blocks_ref.shape[:3]
    highs = entries - 1
    momentum = momentum_ref[...]
    for y in range(ys):
        for low in range(lows):
            for high in range(highs):
                blocks_ref[y, low, high] = params_ref[:, (y * highs + high) * lows + low]
            blocks_ref[y, low, highs] = momentum


def partial_kernel(received_ref, base_ref, packed_ref, momenta_ref):
    sources = received_ref.shape[0]
    peers, blocks, groups = packed_ref.shape[:3]
    momenta_ref[...] = received_ref[:, blocks]
    lows = lax.axis_size("z_lo")
    first = lax.axis_index("y") * (blocks * lows) + lax.axis_index("z_lo")
    for block in range(blocks):
        start = pl.multiple_of((first + block * lows) * BLOCK, BLOCK)
        base = base_ref[:, :, pl.ds(start, BLOCK)].reshape(groups, SUBLANES, BLOCK)
        summed = jnp.zeros(base.shape, jnp.float32)
        for source in range(sources):
            difference = base - received_ref[source, block].astype(jnp.float32)
            largest = jnp.max(jnp.abs(difference), axis=-1, keepdims=True)
            scales = ((largest + EPSILON) / CODE_RANGE).astype(jnp.bfloat16).astype(jnp.float32)
            code_words = (difference / scales).astype(jnp.bfloat16)
            summed = summed + code_words.astype(jnp.float32) * scales
        sent = summed.astype(jnp.bfloat16)
        for peer in range(peers):
            packed_ref[peer, block] = sent


def average_kernel(replicas, packed_ref, received_ref, nearest_ref, averaged_ref, sent_ref, momenta_ref, made_ref, semaphores):
    sources, blocks, groups = packed_ref.shape[:3]
    peers = sent_ref.shape[0]

    def average(block):
        summed = packed_ref[0, block].astype(jnp.float32)
        for source in range(1, sources):
            summed = summed + packed_ref[source, block].astype(jnp.float32)
        return summed / replicas

    squares = jnp.zeros((groups, SUBLANES, BLOCK), jnp.float32)
    for block in range(blocks):
        averaged = average(block)
        squares = squares + averaged * averaged
        made_ref[block * groups : (block + 1) * groups] = averaged.astype(jnp.bfloat16)
    half = groups // 2
    first = jnp.sum(jnp.sum(jnp.sum(squares[:half], axis=0), axis=0, keepdims=True), axis=-1, keepdims=True)
    second = jnp.sum(jnp.sum(jnp.sum(squares[half:], axis=0), axis=0, keepdims=True), axis=-1, keepdims=True)
    tile = (SUBLANES, BLOCK)
    lanes = lax.broadcasted_iota(jnp.int32, tile, 1)
    rows = lax.broadcasted_iota(jnp.int32, tile, 0)
    rest = jnp.where(lanes < BLOCK // 2, first, second)
    pieces = jnp.zeros(tile, jnp.float32)
    for piece in range(3):
        rounded = rest.astype(jnp.bfloat16).astype(jnp.float32)
        pieces = jnp.where(rows == piece, rounded, pieces)
        rest = rest - rounded
    made_ref[blocks * groups] = pieces.astype(jnp.bfloat16)
    writes = [
        pltpu.make_async_copy(made_ref, sent_ref.at[peer], semaphores.at[peer])
        for peer in range(peers)
    ]
    for write in writes:
        write.start()
    momenta_ref[...] = received_ref[:, blocks]
    averaged_ref[...] = average(lax.axis_index("z_hi"))
    for write in writes:
        write.wait()


def sum_kernel(sent_ref, sums_ref):
    sources, tiles = sent_ref.shape[:2]
    total = sent_ref[0, tiles - 1].astype(jnp.float32)
    for source in range(1, sources):
        total = total + sent_ref[source, tiles - 1].astype(jnp.float32)
    sums_ref[...] = jnp.broadcast_to(jnp.sum(total, axis=0, keepdims=True), sums_ref.shape)


def base_kernel(limit, sums_ref, sent_ref, base_ref, averaged_ref, momentum_ref, *refs):
    *momenta_refs, new_base_ref, momentum_next_ref, made_ref, made_momentum_ref, semaphores = refs
    highs = len(momenta_refs)
    groups = averaged_ref.shape[0]
    layers, _, width = base_ref.shape
    lows = lax.axis_size("z_lo")
    ys = sent_ref.shape[0] // lows
    sums = jnp.sum(sums_ref[...], axis=0, keepdims=True)
    factors = []
    for layer in range(layers):
        share = BLOCK // layers
        total = jnp.max(sums[:, layer * share : (layer + 1) * share], axis=-1, keepdims=True)
        factors.append(jnp.minimum(1.0, limit / (jnp.sqrt(total) + EPSILON)))
    rates = [OUTER_RATE * (1.0 + NESTEROV) * factor for factor in factors]
    momentum_rate = OUTER_RATE * NESTEROV * NESTEROV
    for group in range(groups):
        factor = factors[group * layers // groups]
        made_momentum_ref[group] = NESTEROV * momentum_ref[group] + averaged_ref[group] * factor
    chunks = semaphores.shape[0] - 1
    writes = [pltpu.make_async_copy(made_momentum_ref, momentum_next_ref, semaphores.at[chunks])]
    writes[0].start()
    chunk = width // chunks
    mine = lax.axis_index("z_hi")
    for part in range(chunks):
        for y in range(part * ys // chunks, (part + 1) * ys // chunks):
            for shift in range(highs):
                high = lax.rem(mine + shift, highs)
                for low in range(lows):
                    start = pl.multiple_of(((y * highs + high) * lows + low) * BLOCK, BLOCK)
                    columns = pl.ds(start, BLOCK)
                    source = y * lows + low
                    for group in range(groups):
                        layer, half = divmod(group, groups // layers)
                        rows = pl.ds(half * SUBLANES, SUBLANES)
                        averaged = sent_ref[source, high * groups + group].astype(jnp.float32)
                        momentum = momenta_refs[shift][source, group].astype(jnp.float32)
                        step = (averaged * rates[layer] + momentum * momentum_rate).astype(jnp.bfloat16)
                        made_ref[layer, rows, columns] = (
                            base_ref[layer, rows, columns] - step.astype(jnp.float32)
                        )
        columns = pl.ds(part * chunk, chunk)
        write = pltpu.make_async_copy(
            made_ref.at[:, :, columns], new_base_ref.at[:, :, columns], semaphores.at[part]
        )
        write.start()
        writes.append(write)
    for write in writes:
        write.wait()


def per_device(replica_params, outer_base, outer_momentum):
    ys, highs, lows = lax.axis_size("y"), lax.axis_size("z_hi"), lax.axis_size("z_lo")
    xs, cores = lax.axis_size("x"), lax.axis_size("core")
    replicas = ys * highs * lows
    layers, rows, width = outer_base.shape
    groups = layers * rows // SUBLANES
    limit = CLIP_RMS * math.sqrt(rows * xs * cores * width)
    params = pltpu.CompilerParams(vmem_limit_bytes=VMEM_LIMIT)
    tile = (groups, SUBLANES, BLOCK)
    owners = ys * lows
    anywhere = pl.BlockSpec(memory_space=pl.ANY)
    vmem = pl.BlockSpec(memory_space=pltpu.VMEM)
    momentum = outer_momentum.reshape(tile)

    grouped = replica_params.reshape(groups, SUBLANES, replicas, BLOCK).transpose(0, 2, 1, 3)
    blocks = pl.pallas_call(
        split_kernel,
        out_shape=jax.ShapeDtypeStruct((ys, lows, highs + 1, *tile), replica_params.dtype),
        compiler_params=params,
        name="split",
    )(grouped, momentum.astype(jnp.bfloat16))
    received = lax.all_to_all(
        blocks.reshape(owners, highs + 1, *tile), ("y", "z_lo"), 0, 0, tiled=True
    )
    packed, early = pl.pallas_call(
        partial_kernel,
        out_shape=(
            jax.ShapeDtypeStruct((highs, highs, *tile), jnp.bfloat16),
            jax.ShapeDtypeStruct((owners, *tile), jnp.bfloat16),
        ),
        compiler_params=params,
        name="partial",
    )(received, outer_base)
    packed = lax.all_to_all(packed, "z_hi", 0, 0, tiled=True)
    nearest = lax.ppermute(early, "z_hi", [(i, (i - 1) % highs) for i in range(highs)])

    averaged, sent, momenta = pl.pallas_call(
        lambda *refs: average_kernel(replicas, *refs),
        out_shape=(
            jax.ShapeDtypeStruct(tile, jnp.float32),
            jax.ShapeDtypeStruct((owners, highs * groups + 1, SUBLANES, BLOCK), jnp.bfloat16),
            jax.ShapeDtypeStruct((owners, *tile), jnp.bfloat16),
        ),
        out_specs=(vmem, anywhere, vmem),
        scratch_shapes=[
            pltpu.VMEM((highs * groups + 1, SUBLANES, BLOCK), jnp.bfloat16),
            pltpu.SemaphoreType.DMA((owners,)),
        ],
        compiler_params=params,
        name="average",
    )(packed, received, nearest)
    sent = lax.all_to_all(sent, ("y", "z_lo"), 0, 0, tiled=True)
    all_momenta = [momenta, nearest] + [
        lax.ppermute(momenta, "z_hi", [(i, (i - shift) % highs) for i in range(highs)])
        for shift in range(2, highs)
    ]
    shards = xs * cores
    sums = pl.pallas_call(
        sum_kernel,
        out_shape=jax.ShapeDtypeStruct((shards, BLOCK), jnp.float32),
        compiler_params=params,
        name="sum",
    )(sent)
    sums = lax.all_to_all(
        sums.reshape(shards, 1, BLOCK), ("x", "core"), 0, 0, tiled=True
    ).reshape(shards, BLOCK)

    chunks = 8
    new_base, momentum_next = pl.pallas_call(
        lambda *refs: base_kernel(limit, *refs),
        in_specs=[vmem] * (5 + highs),
        out_specs=(anywhere, anywhere),
        out_shape=(
            jax.ShapeDtypeStruct((layers, rows, width), jnp.float32),
            jax.ShapeDtypeStruct(tile, jnp.float32),
        ),
        scratch_shapes=[
            pltpu.VMEM((layers, rows, width), jnp.float32),
            pltpu.VMEM(tile, jnp.float32),
            pltpu.SemaphoreType.DMA((chunks + 1,)),
        ],
        compiler_params=params,
        name="base",
    )(sums, sent, outer_base, averaged, momentum, *all_momenta)
    return (new_base, momentum_next.reshape(outer_momentum.shape))


def solution(mesh):
    replicas, fsdp = mesh.devices.shape
    side = math.isqrt(replicas)
    owners, shards = ("y", "z_hi", "z_lo"), ("x", "core")
    torus = Mesh(
        mesh.devices.reshape(side, side // 2, 2, fsdp // 2, 2), owners + shards
    )
    return jax.shard_map(
        per_device,
        mesh=torus,
        in_specs=(
            P(owners, None, shards, None),
            P(None, shards, None),
            P(None, shards, owners),
        ),
        out_specs=(P(None, shards, None), P(None, shards, owners)),
        check_vma=False,
    )
```
